32 devices in a mesh: gx: 8 (over y, x, core), gy: 4 (over z).
Axes of the slice: x: 2, y: 2, z: 4, core: 2. Of those that a mesh axis runs over, the one named last changes fastest.
Arguments:
- latent: bfloat16 [8, 4, 512, 128], P('gx', 'gy'), may hold values from -6 to 6
- neighbours: int32 [8, 4, 4, 512], P('gx', 'gy'), may hold values from 0 to 511
- top_rows: int32 [8, 4, 2, 256], P('gx', 'gy'), may hold values from 0 to 511
- bottom_rows: int32 [8, 4, 2, 256], P('gx', 'gy'), may hold values from 0 to 511
- edge_top: int32 [8, 4, 2, 1024], P('gx', 'gy'), may hold values from 0 to 255
- edge_bottom: int32 [8, 4, 2, 1024], P('gx', 'gy'), may hold values from 0 to 255
- live_count: int32 [2, 32], P(None, ('gx', 'gy')), may hold values from 1 to 1024, 20480 in all within a row
- edge_weights: bfloat16 [4, 4, 128, 128], replicated, may hold values from -0.5 to 0.5
- node_weights: bfloat16 [4, 3, 128, 128], replicated, may hold values from -0.25 to 0.25
- biases: float32 [4, 3, 128], replicated, may hold values from -3 to 3
Outputs:
- latent_out: bfloat16 [8, 4, 512, 128], P('gx', 'gy')
The draws below stay inside these ranges and needn't reach their ends.
Inputs may be any that keep to these rules, and one draw needn't show every extreme that they name: `live_count`: live cross edges of each domain in each direction, at most 1024; in each direction some domain has exactly 1024.
All inputs are finite; a program needn't handle non-finite values. No bound on the sum of `live_count` on one device may be relied on, other than what follows from the above.
Results may differ from the reference program's by a relative error of at most 0.024.
Values may be sent and summed in bfloat16 or wider, within the bound.
No kernel may reach another device: no remote copies, remote signals or barrier semaphores. Data moves between devices by JAX's collectives and lax.ppermute only.
A program may use at most 64 MiB of HBM per device.

```python
import math
import jax
import jax.numpy as jnp
import numpy as np
from jax import lax

L = 128
K = 4
STEPS = 4
P_SIZE = 512
B = 256
E = 1024
N_GX = 8
N_GY = 4


def set_ends(drawn, stream_key, low, top_value):
    longest = drawn.shape.index(max(drawn.shape))
    spots = []
    for shift in (0, 1):
        where = [jax.random.randint(jax.random.fold_in(stream_key, axis), (), 0, length) for axis, length in enumerate(drawn.shape)]
        where[longest] = (where[longest] + shift) % drawn.shape[longest]
        spots.append(tuple(where))
    return drawn.at[spots[0]].set(low).at[spots[1]].set(top_value)


def shard_levels(stream_key, dims, shards, low, top_value):
    def one(dim, parts):
        steps = jax.random.uniform(jax.random.fold_in(jax.random.fold_in(stream_key, 6), dim), (parts,), jnp.float32, low / len(shards), top_value / len(shards))
        return jnp.repeat(jnp.exp(steps), dims[dim] // parts).reshape((-1,) + (1,) * (len(dims) - dim - 1))

    level = one(*shards[0])
    for cut in shards[1:]:
        level = level * one(*cut)
    return level


def length_profile(count, total, limit, lean):
    loads = [(1 << 20) // math.isqrt(grade ** lean) + 1 for grade in range(2, count + 1)]
    rest, given = total - limit - (count - 1), [1] * (count - 1)
    while rest > 0:
        free = [i for i in range(count - 1) if given[i] < limit]
        pool, left = sum([loads[i] for i in free]), rest
        for i in free:
            addition = min(limit - given[i], max(1, left * loads[i] // pool), rest)
            given[i] = given[i] + addition
            rest = rest - addition
    return np.array([limit] + given)


def ragged_sizes(own_key, number_of, total, limit, skew):
    if number_of == 2:
        one = jax.random.randint(own_key, (), max(1, total - limit), min(limit, total - 1) + 1)
        return jnp.stack([one, total - one])
    sizes = jnp.asarray(length_profile(number_of, total, limit, skew), jnp.int32)
    couples = (number_of - 1) // 2
    source_of, receiver = sizes[1:1 + 2 * couples:2], sizes[2:2 + 2 * couples:2]
    slack = jnp.minimum(source_of - 1, limit - receiver)
    moved = jax.random.randint(jax.random.fold_in(own_key, 1), (couples,), 0, 1 << 20) % (slack + 1)
    sizes = sizes.at[1:1 + 2 * couples:2].set(source_of - moved).at[2:2 + 2 * couples:2].set(receiver + moved)
    return sizes[jax.random.permutation(jax.random.fold_in(own_key, 2), number_of)]


def bell_draw(own_key, extent, spread, reach, split=(), kind=jnp.bfloat16):
    gain = shard_levels(own_key, extent, split, -0.22, 0.18) if split else 1.0
    array = jax.random.normal(own_key, extent, jnp.float32) * spread * gain
    return jnp.minimum(jnp.maximum(array, -reach), reach).astype(kind)


def setup_inputs(seed: int = 0) -> dict:
    keys = jax.random.split(jax.random.key(seed), 11)
    return {
        "latent": bell_draw(keys[0], (N_GX, N_GY, P_SIZE, L), 1.0, 6.0, ((0, 8), (1, 4))),
        "neighbours": set_ends(jax.random.randint(keys[1], (N_GX, N_GY, K, P_SIZE), 0, P_SIZE), jax.random.fold_in(keys[1], 1), 0, P_SIZE - 1).astype(jnp.int32),
        "top_rows": set_ends(jax.random.randint(keys[2], (N_GX, N_GY, 2, B), 0, P_SIZE), jax.random.fold_in(keys[2], 1), 0, P_SIZE - 1).astype(jnp.int32),
        "bottom_rows": set_ends(jax.random.randint(keys[3], (N_GX, N_GY, 2, B), 0, P_SIZE), jax.random.fold_in(keys[3], 1), 0, P_SIZE - 1).astype(jnp.int32),
        "edge_top": set_ends(jax.random.randint(keys[4], (N_GX, N_GY, 2, E), 0, B), jax.random.fold_in(keys[4], 1), 0, B - 1).astype(jnp.int32),
        "edge_bottom": set_ends(jax.random.randint(keys[5], (N_GX, N_GY, 2, E), 0, B), jax.random.fold_in(keys[5], 1), 0, B - 1).astype(jnp.int32),
        "live_count": jax.vmap(lambda own: ragged_sizes(own, N_GX * N_GY, N_GX * N_GY * E * 5 // 8, E, 1))(jax.random.split(keys[6], 2)).reshape((2, N_GX * N_GY)).astype(jnp.int32),
        "edge_weights": bell_draw(keys[7], (STEPS, 4, L, L), L ** -0.5, 0.5),
        "node_weights": bell_draw(keys[8], (STEPS, 3, L, L), (4 * L) ** -0.5, 0.25),
        "biases": bell_draw(keys[9], (STEPS, 3, L), 0.5, 3.0, (), jnp.float32),
    }


def edge_network(summed, w_hidden, w_final, bias_two):
    first = jax.nn.silu(summed).astype(jnp.bfloat16)
    second = jax.nn.silu(jnp.dot(first, w_hidden, preferred_element_type=jnp.float32) + bias_two).astype(jnp.bfloat16)
    return jnp.dot(second, w_final, preferred_element_type=jnp.float32)


def cross_terms(source_rows, target_rows, ends_top, ends_bottom, count, weights, bias_one, bias_two):
    summed = jnp.take(source_rows, ends_top, axis=0) + jnp.take(target_rows, ends_bottom, axis=0) + bias_one
    messages = edge_network(summed, weights[2], weights[3], bias_two)
    live = jnp.arange(ends_top.shape[0], dtype=jnp.int32) < count
    return jnp.where(live[:, None], messages, 0.0)


def roll_grid(values, amount, axis):
    shaped = values.reshape((N_GX, N_GY) + values.shape[1:])
    return jnp.roll(shaped, amount, axis).reshape(values.shape)


def reference(latent, neighbours, top_rows, bottom_rows, edge_top, edge_bottom, live_count, edge_weights, node_weights, biases):
    ndev = N_GX * N_GY
    latent_now = latent.reshape(ndev, P_SIZE, L)
    nbr_all = neighbours.reshape(ndev, K, P_SIZE)
    tops_all = top_rows.reshape(ndev, 2, B)
    bottoms_all = bottom_rows.reshape(ndev, 2, B)
    etop_all = edge_top.reshape(ndev, 2, E)
    ebot_all = edge_bottom.reshape(ndev, 2, E)
    for step in range(STEPS):
        weights = edge_weights[step]
        nodes = node_weights[step]
        bias_one = biases[step, 0]
        bias_two = biases[step, 1]
        bias_node = biases[step, 2]

        def project(rows):
            return (jnp.dot(rows, weights[0], preferred_element_type=jnp.float32),
                    jnp.dot(rows, weights[1], preferred_element_type=jnp.float32))

        proj_src, proj_dst = lax.map(project, latent_now)

        def local_part(items):
            source, target, nbr = items
            flat = nbr.reshape(-1)
            summed = (jnp.take(target, flat, axis=0).reshape(K, P_SIZE, L) + source[None] + bias_one).reshape(K * P_SIZE, L)
            messages = edge_network(summed, weights[2], weights[3], bias_two)
            return messages.reshape(K, P_SIZE, L).sum(0) - jax.ops.segment_sum(messages, flat, num_segments=P_SIZE)

        incoming = lax.map(local_part, (proj_src, proj_dst, nbr_all))
        for direction in range(2):
            tops = tops_all[:, direction]
            bottoms = bottoms_all[:, direction]
            etop = etop_all[:, direction]
            ebot = ebot_all[:, direction]
            bottom_latent = jax.vmap(lambda rows, where: jnp.take(rows, where, axis=0))(latent_now, bottoms)
            upper = roll_grid(bottom_latent, -1, direction)

            def cross_part(items):
                source, up_rows, tp, et, eb, count = items
                target_rows = jnp.dot(up_rows, weights[1], preferred_element_type=jnp.float32)
                return cross_terms(jnp.take(source, tp, axis=0), target_rows, et, eb, count, weights, bias_one, bias_two)

            messages = lax.map(cross_part, (proj_src, upper, tops, etop, ebot, live_count[direction]))
            incoming = incoming + jax.vmap(lambda msg, tp, et: jax.ops.segment_sum(msg, jnp.take(tp, et), num_segments=P_SIZE))(messages, tops, etop)
            returned = jax.vmap(lambda msg, eb: -jax.ops.segment_sum(msg, eb, num_segments=B))(messages, ebot)
            returned = roll_grid(returned, 1, direction)
            incoming = incoming + jax.vmap(lambda back, bt: jax.ops.segment_sum(back, bt, num_segments=P_SIZE))(returned, bottoms)

        def node_update(items):
            rows, arrived = items
            arrived_b = arrived.astype(jnp.bfloat16)
            update = jax.nn.silu(jnp.dot(rows, nodes[0], preferred_element_type=jnp.float32)
                                 + jnp.dot(arrived_b, nodes[1], preferred_element_type=jnp.float32) + bias_node).astype(jnp.bfloat16)
            return (rows.astype(jnp.float32) + jnp.dot(update, nodes[2], preferred_element_type=jnp.float32)).astype(jnp.bfloat16)

        latent_now = lax.map(node_update, (latent_now, incoming))
    return latent_now.reshape(N_GX, N_GY, P_SIZE, L)
```

```python
import functools

import jax
import jax.numpy as jnp
from jax import lax
from jax.experimental import pallas as pl
from jax.experimental.pallas import tpu as pltpu
from jax.sharding import PartitionSpec as P

BF = jnp.bfloat16
F32 = jnp.float32
VMEM = pl.BlockSpec(memory_space=pltpu.VMEM)
SMEM = pl.BlockSpec(memory_space=pltpu.SMEM)


def shifted(block, axis, distance):
    devices = range(lax.axis_size(axis))
    route = [((i - distance) % len(devices), i) for i in devices]
    return lax.ppermute(block, axis, route)


def call(kernel, outs, *operands, in_specs=None, flops=1, name=None):
    moved = sum(o.size * o.dtype.itemsize for o in operands)
    return pl.pallas_call(
        kernel,
        out_shape=outs,
        in_specs=in_specs or [VMEM] * len(operands),
        out_specs=[VMEM] * len(outs),
        compiler_params=pltpu.CompilerParams(vmem_limit_bytes=40 << 20),
        cost_estimate=pl.CostEstimate(flops=flops, bytes_accessed=moved, transcendentals=0),
        name=name,
    )(*operands)


def dot(a, b):
    return jnp.dot(a, b, preferred_element_type=F32)


def half_silu(y):
    return y + y * jnp.tanh(y)


def column_one_hot(row, depth):
    return (lax.broadcasted_iota(jnp.int32, (depth, row.shape[1]), 0) == row).astype(BF)


def column_mask(bit, width):
    return jnp.broadcast_to(bit.astype(F32), (width, bit.shape[1])).T.astype(BF)


def cut(row, half):
    bit = (row >= half).astype(jnp.int32)
    return bit, row - bit * half


def halves(table):
    half = table.shape[0] // 2
    return jnp.concatenate([table[:half], table[half:]], axis=1)


def choose(both, mask):
    width = both.shape[1] // 2
    return jnp.where(mask > 0, both[:, width:], both[:, :width])


def by_half(values, mask):
    upper = values * mask
    return jnp.concatenate([values - upper, upper], axis=1)


def twice_diagonal(w):
    zero = jnp.zeros_like(w)
    return jnp.concatenate(
        [jnp.concatenate([w, zero], axis=1), jnp.concatenate([zero, w], axis=1)], axis=0
    )


def pick_faces(latent, pick_ref, pick_mask_ref, out_refs):
    table = halves(latent)
    for face, out in enumerate(out_refs):
        picked = choose(dot(pick_ref[face], table), pick_mask_ref[face]).astype(BF)
        out[0 : picked.shape[0], :] = picked


def first_kernel(
    latent_ref, tops_ref, bottoms_ref, etop_ref, ebot_ref, live_ref,
    top_x, top_y, bot_x, bot_y, pick_ref, pick_mask_ref,
):
    half = latent_ref.shape[0] // 2
    width = latent_ref.shape[1]
    for face in range(4):
        ref = (tops_ref, bottoms_ref)[face // 2]
        bit, low = cut(ref[face % 2 : face % 2 + 1, :], half)
        pick_ref[face] = column_one_hot(low, half).T
        pick_mask_ref[face] = column_mask(bit, width)
    pick_faces(latent_ref[...], pick_ref, pick_mask_ref, (top_x, top_y, bot_x, bot_y))
    faces = tops_ref.shape[1]
    slots = etop_ref.shape[1]
    lines = slots // width
    for d, out in enumerate((top_x, top_y)):
        live = lax.broadcasted_iota(jnp.int32, (1, slots), 1) < live_ref[d, 0]
        etop = etop_ref[d : d + 1, :].astype(F32)
        ebot = jnp.where(live, ebot_ref[d : d + 1, :], -1).astype(F32)
        rows = [v[:, i * width : (i + 1) * width] for v in (etop, ebot) for i in range(lines)]
        out[faces:, :] = jnp.concatenate(rows, axis=0).astype(BF)


def group(mine, theirs, face, live, sign, half, width):
    faces = face.shape[1]
    here = column_one_hot(mine, faces)
    gather = jnp.concatenate([here, column_one_hot(theirs, faces)], axis=0).T
    bit, low = cut(face, half)
    lines = jnp.concatenate([low, bit, jnp.zeros((6, faces), jnp.int32)], axis=0)
    ends = dot(lines.astype(F32).astype(BF), here).astype(jnp.int32)
    low, bit = ends[0:1, :], ends[1:2, :]
    ones = column_one_hot(jnp.where(live, low, -1), half)
    return gather, ones if sign > 0 else -ones, column_mask(bit, width)


def setup_kernel(
    nbr_ref, tops_ref, etop_ref, ebot_ref, live_ref,
    pick_ref, spread_ref, mask_ref, gather_ref, sum_ref, half_ref,
):
    half = spread_ref.shape[0]
    width = mask_ref.shape[1]
    rows = nbr_ref.shape[1]
    for k in range(nbr_ref.shape[0]):
        here = slice(k * rows, (k + 1) * rows)
        bit, low = cut(nbr_ref[k : k + 1, :], half)
        ones = column_one_hot(low, half)
        pick_ref[here, :] = ones.T
        spread_ref[:, here] = -ones
        mask_ref[here, :] = column_mask(bit, width)
    slots = etop_ref.shape[1]
    for d in range(2):
        live = lax.broadcasted_iota(jnp.int32, (1, slots), 1) < live_ref[d, 0]
        gather_ref[d], sum_ref[d], half_ref[d] = group(
            etop_ref[d : d + 1, :], ebot_ref[d : d + 1, :], tops_ref[d : d + 1, :],
            live, 1, half, width,
        )


def inner_kernel(
    step, latent_ref, tx_ref, ty_ref, bx_ref, by_ref, weights_ref, nodes_ref, biases_ref,
    pick_ref, spread_ref, mask_ref, total_ref, table_ref, fold_ref,
):
    rows, width = latent_ref.shape
    half = rows // 2
    faces = bx_ref.shape[0]
    w01 = jnp.concatenate([weights_ref[step, 0], weights_ref[step, 1]], axis=1) * BF(0.5)
    for face, ref in enumerate((tx_ref, ty_ref, bx_ref, by_ref)):
        end = face // 2
        table_ref[face] = dot(ref[0:faces, :], w01[:, end * width : (end + 1) * width]).astype(BF)
    fold_ref[...] = dot(weights_ref[step, 3], nodes_ref[step, 1]).astype(BF)
    both = dot(latent_ref[...], w01)
    source = both[:, :width] + biases_ref[step, 0:1, :] * 0.5
    table = halves(both[:, width:].astype(BF))
    w2 = twice_diagonal(weights_ref[step, 2] * BF(0.5))
    c1 = biases_ref[step, 1:2, :] * 0.5
    c1 = jnp.concatenate([c1, c1], axis=1)
    fanout = pick_ref.shape[0] // rows
    total = None
    ended = None
    for pair in range(0, fanout, 2):
        first = []
        for k in (pair, pair + 1):
            here = slice(k * rows, (k + 1) * rows)
            target = choose(dot(pick_ref[here, :], table), mask_ref[here, :])
            first.append(half_silu(target + source).astype(BF))
        second = half_silu(dot(jnp.concatenate(first, axis=1), w2) + c1)
        started = second[:, :width] + second[:, width:]
        total = started if total is None else total + started
        second = second.astype(BF)
        for i in range(2):
            k = pair + i
            here = slice(k * rows, (k + 1) * rows)
            values = by_half(second[:, i * width : (i + 1) * width], mask_ref[here, :])
            part = dot(spread_ref[:, here], values)
            ended = part if ended is None else ended + part
    total_ref[0:half, :] = total[0:half] + ended[:, :width]
    total_ref[half:, :] = total[half:] + ended[:, width:]


def cross(step, d, upper, lower, weights_ref, biases_ref, table_ref, groups):
    width = upper.shape[1]
    c0 = biases_ref[step, 0:1, :] * 0.5
    c1 = biases_ref[step, 1:2, :] * 0.5
    c1 = jnp.concatenate([c1, c1], axis=1)
    w2 = twice_diagonal(weights_ref[step, 2] * BF(0.5))
    far = (
        dot(upper, weights_ref[step, 1] * BF(0.5)).astype(BF),
        dot(lower, weights_ref[step, 0] * BF(0.5)).astype(BF),
    )
    first = []
    for i, (gather, _, _) in enumerate(groups):
        table = jnp.concatenate([table_ref[2 * i + d], far[i]], axis=0)
        first.append(half_silu(dot(gather, table) + c0).astype(BF))
    second = half_silu(dot(jnp.concatenate(first, axis=1), w2) + c1).astype(BF)
    total = None
    for i, (_, place, mask) in enumerate(groups):
        part = dot(place, by_half(second[:, i * width : (i + 1) * width], mask))
        total = part if total is None else total + part
    return total


def lower_group(payload_ref, bottoms_ref, d, half):
    faces = bottoms_ref.shape[1]
    width = payload_ref.shape[1]
    sent = payload_ref[faces:, :].astype(F32)
    lines = sent.shape[0] // 2

    def row(start):
        return jnp.concatenate([sent[start + i : start + i + 1, :] for i in range(lines)], axis=1)

    etop = row(0).astype(jnp.int32)
    ebot = row(lines).astype(jnp.int32)
    return group(ebot, etop, bottoms_ref[d : d + 1, :], ebot >= 0, -1, half, width)


def own_group(refs, d):
    return tuple(ref[d] for ref in refs)


def kept_group(refs):
    return tuple(ref[...] for ref in refs)


def x_kernel(step, *refs):
    (total_ref, upper_ref, lower_ref, weights_ref, biases_ref, table_ref) = refs[:6]
    own = refs[6:9]
    rows, width = total_ref.shape
    half = rows // 2
    faces = upper_ref.shape[0]
    if step == 0:
        bottoms_ref, out_ref = refs[9], refs[10]
        keep = refs[11:14]
        for ref, value in zip(keep, lower_group(lower_ref, bottoms_ref, 0, half)):
            ref[...] = value
    else:
        keep, out_ref = refs[9:12], refs[12]
    both = cross(
        step, 0, upper_ref[...], lower_ref[0:faces, :], weights_ref, biases_ref, table_ref,
        (own_group(own, 0), kept_group(keep)),
    )
    out_ref[0:half, :] = total_ref[0:half, :] + both[:, :width]
    out_ref[half:, :] = total_ref[half:, :] + both[:, width:]


def y_kernel(step, last, *refs):
    (total_ref, upper_ref, lower_ref, weights_ref, biases_ref, table_ref) = refs[:6]
    own = refs[6:9]
    latent_ref, nodes_ref, fold_ref = refs[9:12]
    rest = list(refs[12:])
    rows, width = total_ref.shape
    half = rows // 2
    faces = upper_ref.shape[0]
    if step == 0:
        bottoms_ref = rest.pop(0)
    else:
        keep, rest = rest[:3], rest[3:]
    if not last:
        pick_ref, pick_mask_ref, rest = rest[0], rest[1], rest[2:]
    out_ref = rest.pop(0)
    if not last:
        sends, rest = rest[:4], rest[4:]
    if step == 0:
        keep = rest
        for ref, value in zip(keep, lower_group(lower_ref, bottoms_ref, 1, half)):
            ref[...] = value
    both = cross(
        step, 1, upper_ref[...], lower_ref[0:faces, :], weights_ref, biases_ref, table_ref,
        (own_group(own, 1), kept_group(keep)),
    )
    arrived = total_ref[...] + jnp.concatenate([both[:, :width], both[:, width:]], axis=0)
    latent = latent_ref[...]
    matrix = jnp.concatenate([nodes_ref[step, 0], fold_ref[...]], axis=0) * BF(0.5)
    joined = jnp.concatenate([latent, arrived.astype(BF)], axis=1)
    update = half_silu(dot(joined, matrix) + biases_ref[step, 2:3, :] * 0.5).astype(BF)
    latent = (latent.astype(F32) + dot(update, nodes_ref[step, 2])).astype(BF)
    out_ref[...] = latent
    if not last:
        pick_faces(latent, pick_ref, pick_mask_ref, sends)


def local(
    latent,
    neighbours,
    top_rows,
    bottom_rows,
    edge_top,
    edge_bottom,
    live_count,
    edge_weights,
    node_weights,
    biases,
):
    latent_now = latent[0, 0]
    rows, width = latent_now.shape
    half = rows // 2
    nbr = neighbours[0, 0]
    tops = top_rows[0, 0]
    bottoms = bottom_rows[0, 0]
    etop = edge_top[0, 0]
    ebot = edge_bottom[0, 0]
    fanout = nbr.shape[0]
    faces = tops.shape[1]
    slots = etop.shape[1]
    steps = edge_weights.shape[0]
    like = jax.ShapeDtypeStruct
    face = like((faces, width), BF)
    packed = like((faces + 2 * (slots // width), width), BF)
    index_specs = [VMEM] * 4 + [SMEM]
    *sends, pick, pick_mask = call(
        first_kernel,
        [packed, packed, face, face, like((4, faces, half), BF), like((4, faces, width), BF)],
        latent_now, tops, bottoms, etop, ebot, live_count,
        in_specs=[VMEM] + index_specs,
        name="first",
    )
    group_like = [like((slots, 2 * faces), BF), like((half, slots), BF), like((slots, width), BF)]
    inner = call(
        setup_kernel,
        [like((fanout * rows, half), BF), like((half, fanout * rows), BF),
         like((fanout * rows, width), BF)]
        + [like((2,) + g.shape, BF) for g in group_like],
        nbr, tops, etop, ebot, live_count,
        in_specs=index_specs,
        name="setup",
    )
    inner, own = inner[:3], inner[3:]
    kept_x = kept_y = None
    for step in range(steps):
        last = step == steps - 1
        top_x, top_y, bot_x, bot_y = sends
        lower_y = shifted(top_y, "gy", 1)
        upper_y = shifted(bot_y, "gy", -1)
        lower_x = shifted(top_x, "gx", 1)
        upper_x = shifted(bot_x, "gx", -1)
        total, table, fold = call(
            functools.partial(inner_kernel, step),
            [like((rows, width), F32), like((4, faces, width), BF), like((width, width), BF)],
            latent_now, *sends, edge_weights, node_weights, biases, *inner,
            flops=1 << 30,
            name="inner",
        )
        first = step == 0
        total, *made = call(
            functools.partial(x_kernel, step),
            [like((rows, width), F32)] + (group_like if first else []),
            total, upper_x, lower_x, edge_weights, biases, table, *own,
            *([bottoms] if first else kept_x),
            flops=1 << 30,
            name="along_x",
        )
        kept_x = made if first else kept_x
        outs = [like((rows, width), BF)] + ([] if last else [face] * 4)
        latent_now, *made = call(
            functools.partial(y_kernel, step, last),
            outs + (group_like if first else []),
            total, upper_y, lower_y, edge_weights, biases, table, *own,
            latent_now, node_weights, fold,
            *([bottoms] if first else kept_y),
            *([] if last else [pick, pick_mask]),
            flops=1 << 30,
            name="along_y",
        )
        sends, made = made[:4], made[4:]
        kept_y = made if first else kept_y
    return latent_now[None, None]


def solution(mesh):
    return jax.shard_map(
        local,
        mesh=mesh,
        in_specs=(
            P("gx", "gy", None, None),
            P("gx", "gy", None, None),
            P("gx", "gy", None, None),
            P("gx", "gy", None, None),
            P("gx", "gy", None, None),
            P("gx", "gy", None, None),
            P(None, ("gx", "gy")),
            P(),
            P(),
            P(),
        ),
        out_specs=P("gx", "gy", None, None),
        check_vma=False,
    )
```

```python
import functools

import jax
import jax.numpy as jnp
from jax import lax
from jax.experimental import pallas as pl
from jax.experimental.pallas import tpu as pltpu
from jax.sharding import PartitionSpec as P

BF = jnp.bfloat16
F32 = jnp.float32
I32 = jnp.int32
VMEM = pl.BlockSpec(memory_space=pltpu.VMEM)
HBM = pl.BlockSpec(memory_space=pltpu.HBM)


def swapped(block, axis, odd):
    count = lax.axis_size(axis)
    route = []
    for i in range(odd, count, 2):
        j = (i + 1) % count
        route += [(i, j), (j, i)]
    return lax.ppermute(block, axis, route)


def call(kernel, outs, operands, in_specs=None, scratch=(), name=None):
    moved = sum(o.size * o.dtype.itemsize for o in operands)
    return pl.pallas_call(
        kernel,
        out_shape=outs,
        in_specs=in_specs or [VMEM] * len(operands),
        out_specs=[VMEM] * len(outs),
        scratch_shapes=list(scratch),
        compiler_params=pltpu.CompilerParams(vmem_limit_bytes=40 << 20),
        cost_estimate=pl.CostEstimate(flops=1 << 30, bytes_accessed=moved, transcendentals=0),
        name=name,
    )(*operands)


def dot(a, b):
    return jnp.dot(a, b, preferred_element_type=F32)


def half_silu(y):
    return y + y * jnp.tanh(y)


def column_one_hot(row, depth):
    return (lax.broadcasted_iota(I32, (depth, row.shape[1]), 0) == row).astype(BF)


def column_mask(bit, width):
    return jnp.broadcast_to(bit.astype(F32), (width, bit.shape[1])).T.astype(BF)


def cut(row, half):
    bit = (row >= half).astype(I32)
    return bit, row - bit * half


def halves(table):
    half = table.shape[0] // 2
    return jnp.concatenate([table[:half], table[half:]], axis=1)


def choose(both, mask):
    width = both.shape[1] // 2
    return jnp.where(mask > 0, both[:, width:], both[:, :width])


def by_half(values, mask):
    upper = values * mask
    return jnp.concatenate([values - upper, upper], axis=1)


def odd_place():
    return lax.axis_index("gx") % 2, lax.axis_index("gy") % 2


def in_order(odd, first, second):
    turned = odd == 1
    return jnp.where(turned, second, first), jnp.where(turned, first, second)


def pick_faces(latent, pick_ref, pick_mask_ref, out_refs):
    table = halves(latent)
    rows = [
        choose(dot(pick_ref[face], table), pick_mask_ref[face]).astype(BF) for face in range(4)
    ]
    for d, odd in enumerate(odd_place()):
        near, far = in_order(odd, rows[2 * d], rows[2 * d + 1])
        count = near.shape[0]
        out_refs[2 * d][0:count, :] = near
        out_refs[2 * d + 1][0:count, :] = far


def first_kernel(
    latent_hbm, tops_hbm, bottoms_hbm, etop_hbm, ebot_hbm, live_hbm,
    near_x, far_x, near_y, far_y, latent_ref, tops_ref, bottoms_ref, ends_ref,
    pick_ref, pick_mask_ref,
    etop_ref, ebot_ref, live_ref, sems,
):
    moves = [
        pltpu.make_async_copy(src, dst, sems.at[i])
        for i, (src, dst) in enumerate((
            (tops_hbm, tops_ref), (bottoms_hbm, bottoms_ref), (latent_hbm, latent_ref),
            (etop_hbm, etop_ref), (ebot_hbm, ebot_ref), (live_hbm, live_ref),
        ))
    ]
    for move in moves:
        move.start()
    half = latent_ref.shape[0] // 2
    width = latent_ref.shape[1]
    moves[0].wait()
    moves[1].wait()
    for face in range(4):
        d, ref = face // 2, (tops_ref, bottoms_ref)[face % 2]
        bit, low = cut(ref[d : d + 1, :], half)
        pick_ref[face] = column_one_hot(low, half).T
        pick_mask_ref[face] = column_mask(bit, width)
    for move in moves[2:]:
        move.wait()
    sends = (near_x, far_x, near_y, far_y)
    pick_faces(latent_ref[...], pick_ref, pick_mask_ref, sends)
    faces = tops_ref.shape[1]
    slots = etop_ref.shape[1]
    lines = slots // width
    for d in range(2):
        live = lax.broadcasted_iota(I32, (1, slots), 1) < live_ref[d, 0]
        etop = etop_ref[d : d + 1, :].astype(F32)
        ebot = jnp.where(live, ebot_ref[d : d + 1, :], -1).astype(F32)
        rows = [v[:, i * width : (i + 1) * width] for v in (etop, ebot) for i in range(lines)]
        ends = jnp.concatenate(rows, axis=0).astype(BF)
        ends_ref[d] = ends
        sends[2 * d][faces:, :] = ends
        sends[2 * d + 1][faces:, :] = ends


def unpacked(ends):
    ends = ends.astype(F32)
    lines = ends.shape[0] // 2

    def row(start):
        parts = [ends[start + i : start + i + 1, :] for i in range(lines)]
        return jnp.concatenate(parts, axis=1).astype(I32)

    return row(0), row(lines)


def group(mine, theirs, face, live, sign, half, width):
    faces = face.shape[1]
    here = column_one_hot(mine, faces)
    gather = jnp.concatenate([here, column_one_hot(theirs, faces)], axis=0).T
    bit, low = cut(face, half)
    lines = jnp.concatenate([low, bit, jnp.zeros((6, faces), I32)], axis=0)
    ends = dot(lines.astype(F32).astype(BF), here).astype(I32)
    low, bit = ends[0:1, :], ends[1:2, :]
    ones = column_one_hot(jnp.where(live, low, -1), half)
    return gather, ones if sign > 0 else -ones, column_mask(bit, width)


def setup_kernel(
    nbr_hbm, weights_hbm, nodes_hbm, biases_hbm, tops_ref, ends_ref,
    pick_ref, spread_ref, mask_ref, gather_ref, sum_ref, half_ref,
    ends_w_ref, hidden_ref, join_ref, out_w_ref, biases_ref,
    nbr_ref, weights_ref, nodes_ref, raw_biases_ref, sems,
):
    moves = [
        pltpu.make_async_copy(src, dst, sems.at[i])
        for i, (src, dst) in enumerate((
            (nbr_hbm, nbr_ref), (weights_hbm, weights_ref), (nodes_hbm, nodes_ref),
            (biases_hbm, raw_biases_ref),
        ))
    ]
    for move in moves:
        move.start()
    half = spread_ref.shape[0]
    width = mask_ref.shape[1]
    for d in range(2):
        etop, ebot = unpacked(ends_ref[d])
        gather_ref[d], sum_ref[d], half_ref[d] = group(
            etop, ebot, tops_ref[d : d + 1, :], ebot >= 0, 1, half, width
        )
    for move in moves:
        move.wait()
    rows = nbr_ref.shape[1]
    for k in range(nbr_ref.shape[0]):
        here = slice(k * rows, (k + 1) * rows)
        bit, low = cut(nbr_ref[k : k + 1, :], half)
        ones = column_one_hot(low, half)
        pick_ref[here, :] = ones.T
        spread_ref[:, here] = -ones
        mask_ref[here, :] = column_mask(bit, width)
    biases_ref[...] = raw_biases_ref[...] * 0.5
    zero = jnp.zeros((width, width), BF)
    for step in range(weights_ref.shape[0]):
        ends_w_ref[step, 0] = weights_ref[step, 0] * BF(0.5)
        ends_w_ref[step, 1] = weights_ref[step, 1] * BF(0.5)
        hidden = weights_ref[step, 2] * BF(0.5)
        hidden_ref[step] = jnp.concatenate(
            [jnp.concatenate([hidden, zero], axis=1), jnp.concatenate([zero, hidden], axis=1)],
            axis=0,
        )
        fold = dot(weights_ref[step, 3], nodes_ref[step, 1]).astype(BF)
        join_ref[step] = jnp.concatenate([nodes_ref[step, 0], fold], axis=0) * BF(0.5)
        out_w_ref[step] = nodes_ref[step, 2]


def inner_kernel(
    step, latent_ref, near_x, far_x, near_y, far_y, ends_w_ref, hidden_ref, biases_ref,
    pick_ref, spread_ref, mask_ref, total_ref, table_ref,
):
    rows, width = latent_ref.shape
    half = rows // 2
    faces = table_ref.shape[1]
    for d, odd in enumerate(odd_place()):
        near, far = (ref[0:faces, :] for ref in ((near_x, far_x), (near_y, far_y))[d])
        top, bottom = in_order(odd, near, far)
        table_ref[2 * d] = dot(top, ends_w_ref[step, 0]).astype(BF)
        table_ref[2 * d + 1] = dot(bottom, ends_w_ref[step, 1]).astype(BF)
    latent = latent_ref[...]
    source = dot(latent, ends_w_ref[step, 0]) + biases_ref[step, 0:1, :]
    table = halves(dot(latent, ends_w_ref[step, 1]).astype(BF))
    c1 = biases_ref[step, 1:2, :]
    c1 = jnp.concatenate([c1, c1], axis=1)
    fanout = pick_ref.shape[0] // rows
    total = None
    ended = None
    for pair in range(0, fanout, 2):
        first = []
        for k in (pair, pair + 1):
            here = slice(k * rows, (k + 1) * rows)
            target = choose(dot(pick_ref[here, :], table), mask_ref[here, :])
            first.append(half_silu(target + source).astype(BF))
        second = half_silu(dot(jnp.concatenate(first, axis=1), hidden_ref[step]) + c1)
        started = second[:, :width] + second[:, width:]
        total = started if total is None else total + started
        second = second.astype(BF)
        for i in range(2):
            k = pair + i
            here = slice(k * rows, (k + 1) * rows)
            values = by_half(second[:, i * width : (i + 1) * width], mask_ref[here, :])
            part = dot(spread_ref[:, here], values)
            ended = part if ended is None else ended + part
    total_ref[0:half, :] = total[0:half] + ended[:, :width]
    total_ref[half:, :] = total[half:] + ended[:, width:]


def cross(step, d, upper, lower, ends_w_ref, hidden_ref, biases_ref, table_ref, groups):
    width = upper.shape[1]
    c0 = biases_ref[step, 0:1, :]
    c1 = biases_ref[step, 1:2, :]
    c1 = jnp.concatenate([c1, c1], axis=1)
    far = (
        dot(upper, ends_w_ref[step, 1]).astype(BF),
        dot(lower, ends_w_ref[step, 0]).astype(BF),
    )
    first = []
    for i, (gather, _, _) in enumerate(groups):
        table = jnp.concatenate([table_ref[2 * d + i], far[i]], axis=0)
        first.append(half_silu(dot(gather, table) + c0).astype(BF))
    second = half_silu(dot(jnp.concatenate(first, axis=1), hidden_ref[step]) + c1).astype(BF)
    total = None
    for i, (_, place, mask) in enumerate(groups):
        part = dot(place, by_half(second[:, i * width : (i + 1) * width], mask))
        total = part if total is None else total + part
    return total


def lower_group(ends, bottoms_ref, d, half):
    etop, ebot = unpacked(ends)
    return group(ebot, etop, bottoms_ref[d : d + 1, :], ebot >= 0, -1, half, ends.shape[1])


def along(step, d, refs, rows):
    near_ref, far_ref, ends_w_ref, hidden_ref, biases_ref, table_ref = refs[:6]
    own = tuple(ref[d] for ref in refs[6:9])
    half = rows // 2
    faces = table_ref.shape[1]
    upper, lower = in_order(odd_place()[d], near_ref[...], far_ref[...])
    if step == 0:
        bottoms_ref, keep = refs[9], refs[-3:]
        for ref, value in zip(keep, lower_group(lower[faces:], bottoms_ref, d, half)):
            ref[...] = value
        used = 10
    else:
        keep = refs[9:12]
        used = 12
    both = cross(
        step, d, upper[:faces], lower[:faces], ends_w_ref, hidden_ref, biases_ref, table_ref,
        (own, tuple(ref[...] for ref in keep)),
    )
    return both, used


def x_kernel(step, total_ref, *refs):
    rows, width = total_ref.shape
    half = rows // 2
    both, used = along(step, 0, refs, rows)
    out_ref = refs[used]
    out_ref[0:half, :] = total_ref[0:half, :] + both[:, :width]
    out_ref[half:, :] = total_ref[half:, :] + both[:, width:]


def y_kernel(step, last, total_ref, *refs):
    rows, width = total_ref.shape
    both, used = along(step, 1, refs, rows)
    biases_ref = refs[4]
    latent_ref, join_ref, out_w_ref = refs[used : used + 3]
    rest = refs[used + 3 :]
    arrived = total_ref[...] + jnp.concatenate([both[:, :width], both[:, width:]], axis=0)
    latent = latent_ref[...]
    joined = jnp.concatenate([latent, arrived.astype(BF)], axis=1)
    update = half_silu(dot(joined, join_ref[step]) + biases_ref[step, 2:3, :]).astype(BF)
    latent = (latent.astype(F32) + dot(update, out_w_ref[step])).astype(BF)
    if last:
        rest[0][...] = latent
    else:
        pick_ref, pick_mask_ref, out_ref = rest[:3]
        out_ref[...] = latent
        pick_faces(latent, pick_ref, pick_mask_ref, rest[3:7])


def local(
    latent,
    neighbours,
    top_rows,
    bottom_rows,
    edge_top,
    edge_bottom,
    live_count,
    edge_weights,
    node_weights,
    biases,
):
    latent_now = latent[0, 0]
    rows, width = latent_now.shape
    half = rows // 2
    nbr = neighbours[0, 0]
    tops = top_rows[0, 0]
    bottoms = bottom_rows[0, 0]
    etop = edge_top[0, 0]
    ebot = edge_bottom[0, 0]
    fanout = nbr.shape[0]
    faces = tops.shape[1]
    slots = etop.shape[1]
    steps = edge_weights.shape[0]
    like = jax.ShapeDtypeStruct
    face = like((faces, width), BF)
    lines = 2 * (slots // width)
    packed = like((faces + lines, width), BF)
    *sends, latent_now, tops, bottoms, ends, pick, pick_mask = call(
        first_kernel,
        [packed] * 4 + [
            like((rows, width), BF), like(tops.shape, I32), like(tops.shape, I32),
            like((2, lines, width), BF), like((4, faces, half), BF), like((4, faces, width), BF),
        ],
        (latent_now, tops, bottoms, etop, ebot, live_count),
        in_specs=[HBM] * 6,
        scratch=[
            pltpu.VMEM(etop.shape, I32), pltpu.VMEM(etop.shape, I32),
            pltpu.SMEM(live_count.shape, I32), pltpu.SemaphoreType.DMA((6,)),
        ],
        name="first",
    )
    group_like = [
        like((slots, 2 * faces), BF), like((half, slots), BF), like((slots, width), BF)
    ]
    kept_x = kept_y = None
    for step in range(steps):
        first, last = step == 0, step == steps - 1
        near_x, far_x, near_y, far_y = sends
        got_far_y = swapped(far_y, "gy", 1)
        got_near_y = swapped(near_y, "gy", 0)
        got_far_x = swapped(far_x, "gx", 1)
        got_near_x = swapped(near_x, "gx", 0)
        if first:
            made = call(
                setup_kernel,
                [like((fanout * rows, half), BF), like((half, fanout * rows), BF),
                 like((fanout * rows, width), BF)]
                + [like((2,) + g.shape, BF) for g in group_like]
                + [like((steps, 2, width, width), BF), like((steps, 2 * width, 2 * width), BF),
                   like((steps, 2 * width, width), BF), like((steps, width, width), BF),
                   like(biases.shape, F32)],
                (nbr, edge_weights, node_weights, biases, tops, ends),
                in_specs=[HBM] * 4 + [VMEM] * 2,
                scratch=[
                    pltpu.VMEM(nbr.shape, I32), pltpu.VMEM(edge_weights.shape, BF),
                    pltpu.VMEM(node_weights.shape, BF), pltpu.VMEM(biases.shape, F32),
                    pltpu.SemaphoreType.DMA((4,)),
                ],
                name="setup",
            )
            inner, own = made[:3], made[3:6]
            ends_w, hidden, join, out_w, half_biases = made[6:]
            edge_net = (ends_w, hidden, half_biases)
        total, table = call(
            functools.partial(inner_kernel, step),
            [like((rows, width), F32), like((4, faces, width), BF)],
            (latent_now, *sends, *edge_net, *inner),
            name="inner",
        )
        total, *made = call(
            functools.partial(x_kernel, step),
            [like((rows, width), F32)] + (group_like if first else []),
            (total, got_near_x, got_far_x, *edge_net, table, *own,
             *([bottoms] if first else kept_x)),
            name="along_x",
        )
        kept_x = made if first else kept_x
        latent_now, *made = call(
            functools.partial(y_kernel, step, last),
            [like((rows, width), BF)] + ([] if last else [face] * 4)
            + (group_like if first else []),
            (total, got_near_y, got_far_y, *edge_net, table, *own,
             *([bottoms] if first else kept_y), latent_now, join, out_w,
             *([] if last else [pick, pick_mask])),
            name="along_y",
        )
        sends, made = made[:4], made[4:]
        kept_y = made if first else kept_y
    return latent_now[None, None]


def solution(mesh):
    return jax.shard_map(
        local,
        mesh=mesh,
        in_specs=(
            P("gx", "gy", None, None),
            P("gx", "gy", None, None),
            P("gx", "gy", None, None),
            P("gx", "gy", None, None),
            P("gx", "gy", None, None),
            P("gx", "gy", None, None),
            P(None, ("gx", "gy")),
            P(),
            P(),
            P(),
        ),
        out_specs=P("gx", "gy", None, None),
        check_vma=False,
    )
```

```python
import functools

import jax
import jax.numpy as jnp
from jax import lax
from jax.experimental import pallas as pl
from jax.experimental.pallas import tpu as pltpu
from jax.sharding import PartitionSpec as P

BF = jnp.bfloat16
F32 = jnp.float32
I32 = jnp.int32
VMEM = pl.BlockSpec(memory_space=pltpu.VMEM)
HBM = pl.BlockSpec(memory_space=pltpu.HBM)

NEAR_X, FAR_X, NEAR_Y, FAR_Y = range(4)
ORDER = (FAR_Y, FAR_X, NEAR_Y, NEAR_X)
PLACE = tuple(ORDER.index(link) for link in range(4))


def swapped(block, axis, odd):
    count = lax.axis_size(axis)
    route = []
    for i in range(odd, count, 2):
        j = (i + 1) % count
        route += [(i, j), (j, i)]
    return lax.ppermute(block, axis, route)


def call(kernel, outs, operands, in_specs=None, scratch=(), name=None, grant=40 << 20):
    moved = sum(o.size * o.dtype.itemsize for o in operands)
    return pl.pallas_call(
        kernel,
        out_shape=outs,
        in_specs=in_specs or [VMEM] * len(operands),
        out_specs=[VMEM] * len(outs),
        scratch_shapes=list(scratch),
        compiler_params=pltpu.CompilerParams(vmem_limit_bytes=grant),
        cost_estimate=pl.CostEstimate(flops=1 << 30, bytes_accessed=moved, transcendentals=0),
        name=name,
    )(*operands)


def dot(a, b):
    return jnp.dot(a, b, preferred_element_type=F32)


def half_silu(y):
    return y + y * jnp.tanh(y)


def column_one_hot(row, depth):
    return (lax.broadcasted_iota(I32, (depth, row.shape[1]), 0) == row).astype(BF)


def column_mask(bit, width):
    return jnp.broadcast_to(bit.astype(F32), (width, bit.shape[1])).T.astype(BF)


def cut(row, half):
    bit = (row >= half).astype(I32)
    return bit, row - bit * half


def halves(table):
    half = table.shape[0] // 2
    return jnp.concatenate([table[:half], table[half:]], axis=1)


def choose(both, mask):
    width = both.shape[1] // 2
    return jnp.where(mask > 0, both[:, width:], both[:, :width])


def by_half(values, mask):
    upper = values * mask
    return jnp.concatenate([values - upper, upper], axis=1)


def odd_place():
    return lax.axis_index("gx") % 2, lax.axis_index("gy") % 2


def in_order(odd, first, second):
    turned = odd == 1
    return jnp.where(turned, second, first), jnp.where(turned, first, second)


def pick_faces(latent, pick_ref, pick_mask_ref, out_refs):
    table = halves(latent)
    rows = [
        choose(dot(pick_ref[face], table), pick_mask_ref[face]).astype(BF) for face in range(4)
    ]
    for d, odd in enumerate(odd_place()):
        near, far = in_order(odd, rows[2 * d], rows[2 * d + 1])
        count = near.shape[0]
        out_refs[PLACE[2 * d]][0:count, :] = near
        out_refs[PLACE[2 * d + 1]][0:count, :] = far


def first_kernel(
    latent_hbm, tops_hbm, bottoms_hbm, etop_hbm, ebot_hbm, live_hbm,
    send_0, send_1, send_2, send_3, pick_ref, pick_mask_ref,
    latent_ref, tops_ref, bottoms_ref, etop_ref, ebot_ref, live_ref, sems,
):
    moves = [
        pltpu.make_async_copy(src, dst, sems.at[i])
        for i, (src, dst) in enumerate((
            (tops_hbm, tops_ref), (bottoms_hbm, bottoms_ref), (latent_hbm, latent_ref),
            (etop_hbm, etop_ref), (ebot_hbm, ebot_ref), (live_hbm, live_ref),
        ))
    ]
    for move in moves:
        move.start()
    half = latent_ref.shape[0] // 2
    width = latent_ref.shape[1]
    moves[0].wait()
    moves[1].wait()
    for face in range(4):
        d, ref = face // 2, (tops_ref, bottoms_ref)[face % 2]
        bit, low = cut(ref[d : d + 1, :], half)
        pick_ref[face] = column_one_hot(low, half).T
        pick_mask_ref[face] = column_mask(bit, width)
    for move in moves[2:]:
        move.wait()
    sends = (send_0, send_1, send_2, send_3)
    pick_faces(latent_ref[...], pick_ref, pick_mask_ref, sends)
    faces = tops_ref.shape[1]
    slots = etop_ref.shape[1]
    lines = slots // width
    for d in range(2):
        live = lax.broadcasted_iota(I32, (1, slots), 1) < live_ref[0, d]
        etop = etop_ref[d : d + 1, :].astype(F32)
        ebot = jnp.where(live, ebot_ref[d : d + 1, :], -1).astype(F32)
        rows = [v[:, i * width : (i + 1) * width] for v in (etop, ebot) for i in range(lines)]
        ends = jnp.concatenate(rows, axis=0).astype(BF)
        sends[PLACE[2 * d]][faces:, :] = ends
        sends[PLACE[2 * d + 1]][faces:, :] = ends


def unpacked(ends):
    ends = ends.astype(F32)
    lines = ends.shape[0] // 2

    def row(start):
        parts = [ends[start + i : start + i + 1, :] for i in range(lines)]
        return jnp.concatenate(parts, axis=1).astype(I32)

    return row(0), row(lines)


def group(mine, theirs, face, live, sign, half, width):
    faces = face.shape[1]
    here = column_one_hot(mine, faces)
    gather = jnp.concatenate([here, column_one_hot(theirs, faces)], axis=0).T
    bit, low = cut(face, half)
    lines = jnp.concatenate([low, bit, jnp.zeros((6, faces), I32)], axis=0)
    ends = dot(lines.astype(F32).astype(BF), here).astype(I32)
    low, bit = ends[0:1, :], ends[1:2, :]
    ones = column_one_hot(jnp.where(live, low, -1), half)
    return gather, ones if sign > 0 else -ones, column_mask(bit, width)


def setup_kernel(
    tops_hbm, etop_hbm, ebot_hbm, live_hbm, nbr_hbm, weights_hbm, nodes_hbm, biases_hbm,
    pick_ref, spread_ref, mask_ref, gather_ref, sum_ref, half_ref,
    ends_w_ref, hidden_ref, join_ref, out_w_ref, biases_ref,
    tops_ref, etop_ref, ebot_ref, live_ref, nbr_ref, weights_ref, nodes_ref, raw_biases_ref, sems,
):
    moves = [
        pltpu.make_async_copy(src, dst, sems.at[i])
        for i, (src, dst) in enumerate((
            (tops_hbm, tops_ref), (etop_hbm, etop_ref), (ebot_hbm, ebot_ref), (live_hbm, live_ref),
            (nbr_hbm, nbr_ref), (weights_hbm, weights_ref), (nodes_hbm, nodes_ref),
            (biases_hbm, raw_biases_ref),
        ))
    ]
    for move in moves:
        move.start()
    half = spread_ref.shape[0]
    width = mask_ref.shape[1]
    for move in moves[:4]:
        move.wait()
    slots = etop_ref.shape[1]
    for d in range(2):
        live = lax.broadcasted_iota(I32, (1, slots), 1) < live_ref[0, d]
        gather_ref[d], sum_ref[d], half_ref[d] = group(
            etop_ref[d : d + 1, :], ebot_ref[d : d + 1, :], tops_ref[d : d + 1, :],
            live, 1, half, width,
        )
    for move in moves[4:]:
        move.wait()
    rows = nbr_ref.shape[1]
    for k in range(nbr_ref.shape[0]):
        here = slice(k * rows, (k + 1) * rows)
        bit, low = cut(nbr_ref[k : k + 1, :], half)
        ones = column_one_hot(low, half)
        pick_ref[here, :] = ones.T
        spread_ref[:, here] = -ones
        mask_ref[here, :] = column_mask(bit, width)
    biases_ref[...] = raw_biases_ref[...] * 0.5
    zero = jnp.zeros((width, width), BF)
    for step in range(weights_ref.shape[0]):
        ends_w_ref[step, 0] = weights_ref[step, 0] * BF(0.5)
        ends_w_ref[step, 1] = weights_ref[step, 1] * BF(0.5)
        hidden = weights_ref[step, 2] * BF(0.5)
        hidden_ref[step] = jnp.concatenate(
            [jnp.concatenate([hidden, zero], axis=1), jnp.concatenate([zero, hidden], axis=1)],
            axis=0,
        )
        fold = dot(weights_ref[step, 3], nodes_ref[step, 1]).astype(BF)
        join_ref[step] = jnp.concatenate([nodes_ref[step, 0], fold], axis=0) * BF(0.5)
        out_w_ref[step] = nodes_ref[step, 2]


def inner_kernel(
    step, latent_ref, send_0, send_1, send_2, send_3, ends_w_ref, hidden_ref, biases_ref,
    pick_ref, spread_ref, mask_ref, total_ref, table_ref,
):
    rows, width = latent_ref.shape
    half = rows // 2
    faces = table_ref.shape[1]
    sends = (send_0, send_1, send_2, send_3)
    for d, odd in enumerate(odd_place()):
        near, far = (sends[PLACE[2 * d + i]][0:faces, :] for i in range(2))
        top, bottom = in_order(odd, near, far)
        table_ref[2 * d] = dot(top, ends_w_ref[step, 0]).astype(BF)
        table_ref[2 * d + 1] = dot(bottom, ends_w_ref[step, 1]).astype(BF)
    latent = latent_ref[...]
    source = dot(latent, ends_w_ref[step, 0]) + biases_ref[0, step : step + 1, :]
    table = halves(dot(latent, ends_w_ref[step, 1]).astype(BF))
    c1 = biases_ref[1, step : step + 1, :]
    c1 = jnp.concatenate([c1, c1], axis=1)
    fanout = pick_ref.shape[0] // rows
    total = None
    ended = None
    for pair in range(0, fanout, 2):
        first = []
        for k in (pair, pair + 1):
            here = slice(k * rows, (k + 1) * rows)
            target = choose(dot(pick_ref[here, :], table), mask_ref[here, :])
            first.append(half_silu(target + source).astype(BF))
        second = half_silu(dot(jnp.concatenate(first, axis=1), hidden_ref[step]) + c1)
        started = second[:, :width] + second[:, width:]
        total = started if total is None else total + started
        second = second.astype(BF)
        for i in range(2):
            k = pair + i
            here = slice(k * rows, (k + 1) * rows)
            values = by_half(second[:, i * width : (i + 1) * width], mask_ref[here, :])
            part = dot(spread_ref[:, here], values)
            ended = part if ended is None else ended + part
    total_ref[0:half, :] = total[0:half] + ended[:, :width]
    total_ref[half:, :] = total[half:] + ended[:, width:]


def cross(step, d, upper, lower, ends_w_ref, hidden_ref, biases_ref, table_ref, groups):
    width = upper.shape[1]
    c0 = biases_ref[0, step : step + 1, :]
    c1 = biases_ref[1, step : step + 1, :]
    c1 = jnp.concatenate([c1, c1], axis=1)
    far = (
        dot(upper, ends_w_ref[step, 1]).astype(BF),
        dot(lower, ends_w_ref[step, 0]).astype(BF),
    )
    first = []
    for i, (gather, _, _) in enumerate(groups):
        table = jnp.concatenate([table_ref[2 * d + i], far[i]], axis=0)
        first.append(half_silu(dot(gather, table) + c0).astype(BF))
    second = half_silu(dot(jnp.concatenate(first, axis=1), hidden_ref[step]) + c1).astype(BF)
    total = None
    for i, (_, place, mask) in enumerate(groups):
        part = dot(place, by_half(second[:, i * width : (i + 1) * width], mask))
        total = part if total is None else total + part
    return total


def lower_group(ends, bottoms_ref, d, half):
    etop, ebot = unpacked(ends)
    return group(ebot, etop, bottoms_ref[d : d + 1, :], ebot >= 0, -1, half, ends.shape[1])


def along(step, d, refs, rows):
    near_ref, far_ref, ends_w_ref, hidden_ref, biases_ref, table_ref = refs[:6]
    own = tuple(ref[d] for ref in refs[6:9])
    half = rows // 2
    faces = table_ref.shape[1]
    upper, lower = in_order(odd_place()[d], near_ref[...], far_ref[...])
    if step == 0:
        bottoms_ref, keep = refs[9], refs[-3:]
        for ref, value in zip(keep, lower_group(lower[faces:], bottoms_ref, d, half)):
            ref[...] = value
        used = 10
    else:
        keep = refs[9:12]
        used = 12
    both = cross(
        step, d, upper[:faces], lower[:faces], ends_w_ref, hidden_ref, biases_ref, table_ref,
        (own, tuple(ref[...] for ref in keep)),
    )
    return both, used


def x_kernel(step, total_ref, *refs):
    rows, width = total_ref.shape
    half = rows // 2
    both, used = along(step, 0, refs, rows)
    out_ref = refs[used]
    out_ref[0:half, :] = total_ref[0:half, :] + both[:, :width]
    out_ref[half:, :] = total_ref[half:, :] + both[:, width:]


def y_kernel(step, last, total_ref, *refs):
    rows, width = total_ref.shape
    both, used = along(step, 1, refs, rows)
    biases_ref = refs[4]
    latent_ref, join_ref, out_w_ref = refs[used : used + 3]
    rest = refs[used + 3 :]
    arrived = total_ref[...] + jnp.concatenate([both[:, :width], both[:, width:]], axis=0)
    latent = latent_ref[...]
    joined = jnp.concatenate([latent, arrived.astype(BF)], axis=1)
    update = half_silu(dot(joined, join_ref[step]) + biases_ref[2, step : step + 1, :]).astype(BF)
    latent = (latent.astype(F32) + dot(update, out_w_ref[step])).astype(BF)
    if last:
        rest[0][...] = latent
    else:
        pick_ref, pick_mask_ref, out_ref = rest[:3]
        out_ref[...] = latent
        pick_faces(latent, pick_ref, pick_mask_ref, rest[3:7])


def local(
    latent,
    neighbours,
    top_rows,
    bottom_rows,
    edge_top,
    edge_bottom,
    live_count,
    edge_weights,
    node_weights,
    biases,
):
    latent_now = latent[0, 0]
    rows, width = latent_now.shape
    half = rows // 2
    nbr = neighbours[0, 0]
    tops = top_rows[0, 0]
    bottoms = bottom_rows[0, 0]
    etop = edge_top[0, 0]
    ebot = edge_bottom[0, 0]
    live = live_count.T
    bias_rows = jnp.swapaxes(biases, 0, 1)
    fanout = nbr.shape[0]
    faces = tops.shape[1]
    slots = etop.shape[1]
    steps = edge_weights.shape[0]
    like = jax.ShapeDtypeStruct
    face = like((faces, width), BF)
    lines = 2 * (slots // width)
    packed = like((faces + lines, width), BF)
    *sends, pick, pick_mask = call(
        first_kernel,
        [packed] * 4 + [like((4, faces, half), BF), like((4, faces, width), BF)],
        (latent_now, tops, bottoms, etop, ebot, live),
        in_specs=[HBM] * 6,
        scratch=[
            pltpu.VMEM((rows, width), BF), pltpu.VMEM(tops.shape, I32),
            pltpu.VMEM(tops.shape, I32), pltpu.VMEM(etop.shape, I32), pltpu.VMEM(etop.shape, I32),
            pltpu.SMEM(live.shape, I32), pltpu.SemaphoreType.DMA((6,)),
        ],
        name="first",
        grant=54 << 20,
    )
    group_like = [
        like((slots, 2 * faces), BF), like((half, slots), BF), like((slots, width), BF)
    ]
    kept_x = kept_y = None
    for step in range(steps):
        first, last = step == 0, step == steps - 1
        near_x, far_x, near_y, far_y = (sends[place] for place in PLACE)
        got_far_y = swapped(far_y, "gy", 1)
        got_near_y = swapped(near_y, "gy", 0)
        got_far_x = swapped(far_x, "gx", 1)
        got_near_x = swapped(near_x, "gx", 0)
        if first:
            made = call(
                setup_kernel,
                [like((fanout * rows, half), BF), like((half, fanout * rows), BF),
                 like((fanout * rows, width), BF)]
                + [like((2,) + g.shape, BF) for g in group_like]
                + [like((steps, 2, width, width), BF), like((steps, 2 * width, 2 * width), BF),
                   like((steps, 2 * width, width), BF), like((steps, width, width), BF),
                   like(bias_rows.shape, F32)],
                (tops, etop, ebot, live, nbr, edge_weights, node_weights, bias_rows),
                in_specs=[HBM] * 8,
                scratch=[
                    pltpu.VMEM(tops.shape, I32), pltpu.VMEM(etop.shape, I32),
                    pltpu.VMEM(etop.shape, I32), pltpu.SMEM(live.shape, I32),
                    pltpu.VMEM(nbr.shape, I32), pltpu.VMEM(edge_weights.shape, BF),
                    pltpu.VMEM(node_weights.shape, BF), pltpu.VMEM(bias_rows.shape, F32),
                    pltpu.SemaphoreType.DMA((8,)),
                ],
                name="setup",
            )
            inner, own = made[:3], made[3:6]
            ends_w, hidden, join, out_w, half_biases = made[6:]
            edge_net = (ends_w, hidden, half_biases)
        total, table = call(
            functools.partial(inner_kernel, step),
            [like((rows, width), F32), like((4, faces, width), BF)],
            (latent_now, *sends, *edge_net, *inner),
            name="inner",
        )
        total, *made = call(
            functools.partial(x_kernel, step),
            [like((rows, width), F32)] + (group_like if first else []),
            (total, got_near_x, got_far_x, *edge_net, table, *own,
             *([bottoms] if first else kept_x)),
            name="along_x",
        )
        kept_x = made if first else kept_x
        latent_now, *made = call(
            functools.partial(y_kernel, step, last),
            [like((rows, width), BF)] + ([] if last else [face] * 4)
            + (group_like if first else []),
            (total, got_near_y, got_far_y, *edge_net, table, *own,
             *([bottoms] if first else kept_y), latent_now, join, out_w,
             *([] if last else [pick, pick_mask])),
            name="along_y",
        )
        sends, made = made[:4], made[4:]
        kept_y = made if first else kept_y
    return latent_now[None, None]


def solution(mesh):
    return jax.shard_map(
        local,
        mesh=mesh,
        in_specs=(
            P("gx", "gy", None, None),
            P("gx", "gy", None, None),
            P("gx", "gy", None, None),
            P("gx", "gy", None, None),
            P("gx", "gy", None, None),
            P("gx", "gy", None, None),
            P(None, ("gx", "gy")),
            P(),
            P(),
            P(),
        ),
        out_specs=P("gx", "gy", None, None),
        check_vma=False,
    )
```

```python
import functools

import jax
import jax.numpy as jnp
from jax import lax
from jax.experimental import pallas as pl
from jax.experimental.pallas import tpu as pltpu
from jax.sharding import PartitionSpec as P

BF = jnp.bfloat16
F32 = jnp.float32
I32 = jnp.int32
VMEM = pl.BlockSpec(memory_space=pltpu.VMEM)
SMEM = pl.BlockSpec(memory_space=pltpu.SMEM)
HBM = pl.BlockSpec(memory_space=pltpu.HBM)

NEAR_X, FAR_X, NEAR_Y, FAR_Y = range(4)
ORDER = (FAR_Y, FAR_X, NEAR_Y, NEAR_X)
PLACE = tuple(ORDER.index(link) for link in range(4))


def swapped(block, axis, odd):
    count = lax.axis_size(axis)
    route = []
    for i in range(odd, count, 2):
        j = (i + 1) % count
        route += [(i, j), (j, i)]
    return lax.ppermute(block, axis, route)


def call(kernel, outs, operands, in_specs=None, scratch=(), name=None, grant=40 << 20):
    moved = sum(o.size * o.dtype.itemsize for o in operands)
    return pl.pallas_call(
        kernel,
        out_shape=outs,
        in_specs=in_specs or [VMEM] * len(operands),
        out_specs=[VMEM] * len(outs),
        scratch_shapes=list(scratch),
        compiler_params=pltpu.CompilerParams(vmem_limit_bytes=grant),
        cost_estimate=pl.CostEstimate(flops=1 << 30, bytes_accessed=moved, transcendentals=0),
        name=name,
    )(*operands)


def dot(a, b):
    return jnp.dot(a, b, preferred_element_type=F32)


def half_silu(y):
    return y + y * jnp.tanh(y)


def column_one_hot(row, depth):
    depths = lax.broadcasted_iota(jnp.int16, (depth, row.shape[1]), 0)
    return jnp.where(depths == row.astype(jnp.int16), BF(1), BF(0))


def column_mask(bit, width):
    return jnp.broadcast_to(bit.astype(F32).astype(BF), (width, bit.shape[1])).T


def cut(row, half):
    bit = (row >= half).astype(I32)
    return bit, row - bit * half


def halves(table):
    half = table.shape[0] // 2
    return jnp.concatenate([table[:half], table[half:]], axis=1)


def choose(both, mask):
    width = both.shape[1] // 2
    return jnp.where(mask > 0, both[:, width:], both[:, :width])


def by_half(values, mask):
    upper = values * mask
    return jnp.concatenate([values - upper, upper], axis=1)


def odd_place():
    return lax.axis_index("gx") % 2, lax.axis_index("gy") % 2


def in_order(odd, first, second):
    turned = odd == 1
    return jnp.where(turned, second, first), jnp.where(turned, first, second)


def pick_faces(latent, pick_ref, pick_mask_ref, out_refs):
    table = halves(latent)
    rows = [
        choose(dot(pick_ref[face], table), pick_mask_ref[face]).astype(BF) for face in range(4)
    ]
    for d, odd in enumerate(odd_place()):
        near, far = in_order(odd, rows[2 * d], rows[2 * d + 1])
        count = near.shape[0]
        out_refs[PLACE[2 * d]][0:count, :] = near
        out_refs[PLACE[2 * d + 1]][0:count, :] = far


def first_kernel(
    latent_hbm, tops_hbm, bottoms_hbm, etop_hbm, ebot_hbm, live_hbm,
    send_0, send_1, send_2, send_3, pick_ref, pick_mask_ref,
    latent_ref, tops_ref, bottoms_ref, etop_ref, ebot_ref, live_ref, sems,
):
    moves = [
        pltpu.make_async_copy(src, dst, sems.at[i])
        for i, (src, dst) in enumerate((
            (tops_hbm, tops_ref), (bottoms_hbm, bottoms_ref), (latent_hbm, latent_ref),
            (etop_hbm, etop_ref), (ebot_hbm, ebot_ref), (live_hbm, live_ref),
        ))
    ]
    for move in moves:
        move.start()
    half = latent_ref.shape[0] // 2
    width = latent_ref.shape[1]
    moves[0].wait()
    moves[1].wait()
    for face in range(4):
        d, ref = face // 2, (tops_ref, bottoms_ref)[face % 2]
        bit, low = cut(ref[d : d + 1, :], half)
        pick_ref[face] = column_one_hot(low, half).T
        pick_mask_ref[face] = column_mask(bit, width)
    for move in moves[2:]:
        move.wait()
    sends = (send_0, send_1, send_2, send_3)
    pick_faces(latent_ref[...], pick_ref, pick_mask_ref, sends)
    faces = tops_ref.shape[1]
    slots = etop_ref.shape[1]
    lines = slots // width
    for d in range(2):
        live = lax.broadcasted_iota(I32, (1, slots), 1) < live_ref[0, d]
        etop = etop_ref[d : d + 1, :].astype(F32)
        ebot = jnp.where(live, ebot_ref[d : d + 1, :], -1).astype(F32)
        rows = [v[:, i * width : (i + 1) * width] for v in (etop, ebot) for i in range(lines)]
        ends = jnp.concatenate(rows, axis=0).astype(BF)
        sends[PLACE[2 * d]][faces:, :] = ends
        sends[PLACE[2 * d + 1]][faces:, :] = ends


def unpacked(ends):
    ends = ends.astype(F32)
    lines = ends.shape[0] // 2

    def row(start):
        parts = [ends[start + i : start + i + 1, :] for i in range(lines)]
        return jnp.concatenate(parts, axis=1).astype(I32)

    return row(0), row(lines)


def group(mine, theirs, face, live, sign, half, width):
    faces = face.shape[1]
    here = column_one_hot(mine, faces)
    gather = jnp.concatenate([here, column_one_hot(theirs, faces)], axis=0).T
    bit, low = cut(face, half)
    lines = jnp.concatenate([low, bit, jnp.zeros((6, faces), I32)], axis=0)
    ends = dot(lines.astype(F32).astype(BF), here).astype(I32)
    low, bit = ends[0:1, :], ends[1:2, :]
    ones = column_one_hot(jnp.where(live, low, -1), half)
    return gather, ones if sign > 0 else -ones, column_mask(bit, width)


def setup_kernel(
    tops_ref, etop_ref, ebot_ref, live_ref, nbr_ref, weights_ref, nodes_ref, raw_biases_ref,
    pick_ref, spread_ref, mask_ref, gather_ref, sum_ref, half_ref,
    ends_w_ref, hidden_ref, join_ref, out_w_ref, biases_ref,
):
    half = spread_ref.shape[0]
    width = mask_ref.shape[1]
    slots = etop_ref.shape[1]
    for d in range(2):
        live = lax.broadcasted_iota(I32, (1, slots), 1) < live_ref[0, d]
        gather_ref[d], sum_ref[d], half_ref[d] = group(
            etop_ref[d : d + 1, :], ebot_ref[d : d + 1, :], tops_ref[d : d + 1, :],
            live, 1, half, width,
        )
    rows = nbr_ref.shape[1]
    for k in range(nbr_ref.shape[0]):
        here = slice(k * rows, (k + 1) * rows)
        bit, low = cut(nbr_ref[k : k + 1, :], half)
        ones = column_one_hot(low, half)
        pick_ref[here, :] = ones.T
        spread_ref[:, here] = -ones
        mask_ref[here, :] = column_mask(bit, width)
    biases_ref[...] = raw_biases_ref[...] * 0.5
    zero = jnp.zeros((width, width), BF)
    for step in range(weights_ref.shape[0]):
        ends_w_ref[step, 0] = weights_ref[step, 0] * BF(0.5)
        ends_w_ref[step, 1] = weights_ref[step, 1] * BF(0.5)
        hidden = weights_ref[step, 2] * BF(0.5)
        hidden_ref[step] = jnp.concatenate(
            [jnp.concatenate([hidden, zero], axis=1), jnp.concatenate([zero, hidden], axis=1)],
            axis=0,
        )
        fold = dot(weights_ref[step, 3], nodes_ref[step, 1]).astype(BF)
        join_ref[step] = jnp.concatenate([nodes_ref[step, 0], fold], axis=0) * BF(0.5)
        out_w_ref[step] = nodes_ref[step, 2]


def inner_kernel(
    step, latent_ref, send_0, send_1, send_2, send_3, ends_w_ref, hidden_ref, biases_ref,
    pick_ref, spread_ref, mask_ref, total_ref, table_ref,
):
    rows, width = latent_ref.shape
    half = rows // 2
    faces = table_ref.shape[1]
    sends = (send_0, send_1, send_2, send_3)
    for d, odd in enumerate(odd_place()):
        near, far = (sends[PLACE[2 * d + i]][0:faces, :] for i in range(2))
        top, bottom = in_order(odd, near, far)
        table_ref[2 * d] = dot(top, ends_w_ref[step, 0]).astype(BF)
        table_ref[2 * d + 1] = dot(bottom, ends_w_ref[step, 1]).astype(BF)
    latent = latent_ref[...]
    source = dot(latent, ends_w_ref[step, 0]) + biases_ref[0, step : step + 1, :]
    table = halves(dot(latent, ends_w_ref[step, 1]).astype(BF))
    c1 = biases_ref[1, step : step + 1, :]
    c1 = jnp.concatenate([c1, c1], axis=1)
    fanout = pick_ref.shape[0] // rows
    total = None
    ended = None
    for pair in range(0, fanout, 2):
        first = []
        for k in (pair, pair + 1):
            here = slice(k * rows, (k + 1) * rows)
            target = choose(dot(pick_ref[here, :], table), mask_ref[here, :])
            first.append(half_silu(target + source).astype(BF))
        second = half_silu(dot(jnp.concatenate(first, axis=1), hidden_ref[step]) + c1)
        started = second[:, :width] + second[:, width:]
        total = started if total is None else total + started
        second = second.astype(BF)
        for i in range(2):
            k = pair + i
            here = slice(k * rows, (k + 1) * rows)
            values = by_half(second[:, i * width : (i + 1) * width], mask_ref[here, :])
            part = dot(spread_ref[:, here], values)
            ended = part if ended is None else ended + part
    total_ref[0:half, :] = total[0:half] + ended[:, :width]
    total_ref[half:, :] = total[half:] + ended[:, width:]


def cross(step, d, upper, lower, ends_w_ref, hidden_ref, biases_ref, table_ref, groups):
    width = upper.shape[1]
    c0 = biases_ref[0, step : step + 1, :]
    c1 = biases_ref[1, step : step + 1, :]
    c1 = jnp.concatenate([c1, c1], axis=1)
    far = (
        dot(upper, ends_w_ref[step, 1]).astype(BF),
        dot(lower, ends_w_ref[step, 0]).astype(BF),
    )
    first = []
    for i, (gather, _, _) in enumerate(groups):
        table = jnp.concatenate([table_ref[2 * d + i], far[i]], axis=0)
        first.append(half_silu(dot(gather, table) + c0).astype(BF))
    second = half_silu(dot(jnp.concatenate(first, axis=1), hidden_ref[step]) + c1).astype(BF)
    total = None
    for i, (_, place, mask) in enumerate(groups):
        part = dot(place, by_half(second[:, i * width : (i + 1) * width], mask))
        total = part if total is None else total + part
    return total


def lower_group(ends, bottoms_ref, d, half):
    etop, ebot = unpacked(ends)
    return group(ebot, etop, bottoms_ref[d : d + 1, :], ebot >= 0, -1, half, ends.shape[1])


def along(step, d, refs, rows):
    near_ref, far_ref, ends_w_ref, hidden_ref, biases_ref, table_ref = refs[:6]
    own = tuple(ref[d] for ref in refs[6:9])
    half = rows // 2
    faces = table_ref.shape[1]
    upper, lower = in_order(odd_place()[d], near_ref[...], far_ref[...])
    if step == 0:
        bottoms_ref, keep = refs[9], refs[-3:]
        for ref, value in zip(keep, lower_group(lower[faces:], bottoms_ref, d, half)):
            ref[...] = value
        used = 10
    else:
        keep = refs[9:12]
        used = 12
    both = cross(
        step, d, upper[:faces], lower[:faces], ends_w_ref, hidden_ref, biases_ref, table_ref,
        (own, tuple(ref[...] for ref in keep)),
    )
    return both, used


def x_kernel(step, total_ref, *refs):
    rows, width = total_ref.shape
    half = rows // 2
    both, used = along(step, 0, refs, rows)
    out_ref = refs[used]
    out_ref[0:half, :] = total_ref[0:half, :] + both[:, :width]
    out_ref[half:, :] = total_ref[half:, :] + both[:, width:]


def y_kernel(step, last, total_ref, *refs):
    rows, width = total_ref.shape
    both, used = along(step, 1, refs, rows)
    biases_ref = refs[4]
    latent_ref, join_ref, out_w_ref = refs[used : used + 3]
    rest = refs[used + 3 :]
    arrived = total_ref[...] + jnp.concatenate([both[:, :width], both[:, width:]], axis=0)
    latent = latent_ref[...]
    joined = jnp.concatenate([latent, arrived.astype(BF)], axis=1)
    update = half_silu(dot(joined, join_ref[step]) + biases_ref[2, step : step + 1, :]).astype(BF)
    latent = (latent.astype(F32) + dot(update, out_w_ref[step])).astype(BF)
    if last:
        rest[0][...] = latent
    else:
        pick_ref, pick_mask_ref, out_ref = rest[:3]
        out_ref[...] = latent
        pick_faces(latent, pick_ref, pick_mask_ref, rest[3:7])


def local(
    latent,
    neighbours,
    top_rows,
    bottom_rows,
    edge_top,
    edge_bottom,
    live_count,
    edge_weights,
    node_weights,
    biases,
):
    latent_now = latent[0, 0]
    rows, width = latent_now.shape
    half = rows // 2
    nbr = neighbours[0, 0]
    tops = top_rows[0, 0]
    bottoms = bottom_rows[0, 0]
    etop = edge_top[0, 0]
    ebot = edge_bottom[0, 0]
    live = live_count.T
    bias_rows = jnp.swapaxes(biases, 0, 1)
    fanout = nbr.shape[0]
    faces = tops.shape[1]
    slots = etop.shape[1]
    steps = edge_weights.shape[0]
    like = jax.ShapeDtypeStruct
    face = like((faces, width), BF)
    lines = 2 * (slots // width)
    packed = like((faces + lines, width), BF)
    *sends, pick, pick_mask = call(
        first_kernel,
        [packed] * 4 + [like((4, faces, half), BF), like((4, faces, width), BF)],
        (latent_now, tops, bottoms, etop, ebot, live),
        in_specs=[HBM] * 6,
        scratch=[
            pltpu.VMEM((rows, width), BF), pltpu.VMEM(tops.shape, I32),
            pltpu.VMEM(tops.shape, I32), pltpu.VMEM(etop.shape, I32), pltpu.VMEM(etop.shape, I32),
            pltpu.SMEM(live.shape, I32), pltpu.SemaphoreType.DMA((6,)),
        ],
        name="first",
        grant=54 << 20,
    )
    group_like = [
        like((slots, 2 * faces), BF), like((half, slots), BF), like((slots, width), BF)
    ]
    kept_x = kept_y = None
    for step in range(steps):
        first, last = step == 0, step == steps - 1
        near_x, far_x, near_y, far_y = (sends[place] for place in PLACE)
        got_far_y = swapped(far_y, "gy", 1)
        got_near_y = swapped(near_y, "gy", 0)
        got_far_x = swapped(far_x, "gx", 1)
        got_near_x = swapped(near_x, "gx", 0)
        if first:
            made = call(
                setup_kernel,
                [like((fanout * rows, half), BF), like((half, fanout * rows), BF),
                 like((fanout * rows, width), BF)]
                + [like((2,) + g.shape, BF) for g in group_like]
                + [like((steps, 2, width, width), BF), like((steps, 2 * width, 2 * width), BF),
                   like((steps, 2 * width, width), BF), like((steps, width, width), BF),
                   like(bias_rows.shape, F32)],
                (tops, etop, ebot, live, nbr, edge_weights, node_weights, bias_rows),
                in_specs=[VMEM] * 3 + [SMEM] + [VMEM] * 4,
                name="setup",
            )
            inner, own = made[:3], made[3:6]
            ends_w, hidden, join, out_w, half_biases = made[6:]
            edge_net = (ends_w, hidden, half_biases)
        total, table = call(
            functools.partial(inner_kernel, step),
            [like((rows, width), F32), like((4, faces, width), BF)],
            (latent_now, *sends, *edge_net, *inner),
            name="inner",
        )
        total, *made = call(
            functools.partial(x_kernel, step),
            [like((rows, width), F32)] + (group_like if first else []),
            (total, got_near_x, got_far_x, *edge_net, table, *own,
             *([bottoms] if first else kept_x)),
            name="along_x",
        )
        kept_x = made if first else kept_x
        latent_now, *made = call(
            functools.partial(y_kernel, step, last),
            [like((rows, width), BF)] + ([] if last else [face] * 4)
            + (group_like if first else []),
            (total, got_near_y, got_far_y, *edge_net, table, *own,
             *([bottoms] if first else kept_y), latent_now, join, out_w,
             *([] if last else [pick, pick_mask])),
            name="along_y",
        )
        sends, made = made[:4], made[4:]
        kept_y = made if first else kept_y
    return latent_now[None, None]


def solution(mesh):
    return jax.shard_map(
        local,
        mesh=mesh,
        in_specs=(
            P("gx", "gy", None, None),
            P("gx", "gy", None, None),
            P("gx", "gy", None, None),
            P("gx", "gy", None, None),
            P("gx", "gy", None, None),
            P("gx", "gy", None, None),
            P(None, ("gx", "gy")),
            P(),
            P(),
            P(),
        ),
        out_specs=P("gx", "gy", None, None),
        check_vma=False,
    )
```

```python
import functools

import jax
import jax.numpy as jnp
from jax import lax
from jax.experimental import pallas as pl
from jax.experimental.pallas import tpu as pltpu
from jax.sharding import PartitionSpec as P

BF = jnp.bfloat16
F32 = jnp.float32
I32 = jnp.int32
VMEM = pl.BlockSpec(memory_space=pltpu.VMEM)
SMEM = pl.BlockSpec(memory_space=pltpu.SMEM)
HBM = pl.BlockSpec(memory_space=pltpu.HBM)

CUT = 128

NEAR_X, FAR_X, NEAR_Y, FAR_Y = range(4)
ORDER = (FAR_Y, FAR_X, NEAR_Y, NEAR_X)
PLACE = tuple(ORDER.index(link) for link in range(4))


def swapped(block, axis, odd):
    count = lax.axis_size(axis)
    route = []
    for i in range(odd, count, 2):
        j = (i + 1) % count
        route += [(i, j), (j, i)]
    return lax.ppermute(block, axis, route)


def call(kernel, outs, operands, in_specs=None, scratch=(), name=None, grant=40 << 20):
    moved = sum(o.size * o.dtype.itemsize for o in operands)
    return pl.pallas_call(
        kernel,
        out_shape=outs,
        in_specs=in_specs or [VMEM] * len(operands),
        out_specs=[VMEM] * len(outs),
        scratch_shapes=list(scratch),
        compiler_params=pltpu.CompilerParams(vmem_limit_bytes=grant),
        cost_estimate=pl.CostEstimate(flops=1 << 30, bytes_accessed=moved, transcendentals=0),
        name=name,
    )(*operands)


def dot(a, b):
    return jnp.dot(a, b, preferred_element_type=F32)


def half_silu(y):
    return y + y * jnp.tanh(y)


def column_one_hot(row, depth):
    depths = lax.broadcasted_iota(jnp.int16, (depth, row.shape[1]), 0)
    return jnp.where(depths == row.astype(jnp.int16), BF(1), BF(0))


def column_mask(bit, width):
    return jnp.broadcast_to(bit.astype(F32).astype(BF), (width, bit.shape[1])).T


def cut(row, half):
    bit = (row >= half).astype(I32)
    return bit, row - bit * half


def halves(table):
    half = table.shape[0] // 2
    return jnp.concatenate([table[:half], table[half:]], axis=1)


def choose(both, mask):
    width = both.shape[1] // 2
    return jnp.where(mask > 0, both[:, width:], both[:, :width])


def by_half(values, mask):
    upper = values * mask
    return jnp.concatenate([values - upper, upper], axis=1)


def odd_place():
    return lax.axis_index("gx") % 2, lax.axis_index("gy") % 2


def in_order(odd, first, second):
    turned = odd == 1
    return jnp.where(turned, second, first), jnp.where(turned, first, second)


def pick_faces(latent, pick_ref, pick_mask_ref, out_refs):
    table = halves(latent)
    rows = [
        choose(dot(pick_ref[face], table), pick_mask_ref[face]).astype(BF) for face in range(4)
    ]
    for d, odd in enumerate(odd_place()):
        near, far = in_order(odd, rows[2 * d], rows[2 * d + 1])
        count = near.shape[0]
        out_refs[PLACE[2 * d]][0:count, :] = near
        out_refs[PLACE[2 * d + 1]][0:count, :] = far


def first_kernel(
    latent_hbm, tops_hbm, bottoms_hbm, etop_hbm, ebot_hbm, live_hbm,
    send_0, send_1, send_2, send_3, pick_ref, pick_mask_ref,
    latent_ref, tops_ref, bottoms_ref, etop_ref, ebot_ref, live_ref, sems,
):
    moves = [
        pltpu.make_async_copy(src, dst, sems.at[i])
        for i, (src, dst) in enumerate((
            (tops_hbm, tops_ref), (bottoms_hbm, bottoms_ref), (latent_hbm, latent_ref),
            (etop_hbm, etop_ref), (ebot_hbm, ebot_ref), (live_hbm, live_ref),
        ))
    ]
    for move in moves:
        move.start()
    half = latent_ref.shape[0] // 2
    width = latent_ref.shape[1]
    moves[0].wait()
    moves[1].wait()
    for face in range(4):
        d, ref = face // 2, (tops_ref, bottoms_ref)[face % 2]
        bit, low = cut(ref[d : d + 1, :], half)
        pick_ref[face] = column_one_hot(low, half).T
        pick_mask_ref[face] = column_mask(bit, width)
    for move in moves[2:]:
        move.wait()
    sends = (send_0, send_1, send_2, send_3)
    pick_faces(latent_ref[...], pick_ref, pick_mask_ref, sends)
    faces = tops_ref.shape[1]
    slots = etop_ref.shape[1]
    lines = slots // width
    for d in range(2):
        live = lax.broadcasted_iota(I32, (1, slots), 1) < live_ref[0, d]
        etop = etop_ref[d : d + 1, :].astype(F32)
        ebot = jnp.where(live, ebot_ref[d : d + 1, :], -1).astype(F32)
        rows = [v[:, i * width : (i + 1) * width] for v in (etop, ebot) for i in range(lines)]
        ends = jnp.concatenate(rows, axis=0).astype(BF)
        sends[PLACE[2 * d]][faces:, :] = ends
        sends[PLACE[2 * d + 1]][faces:, :] = ends


def unpacked(ends):
    ends = ends.astype(F32)
    lines = ends.shape[0] // 2

    def row(start):
        parts = [ends[start + i : start + i + 1, :] for i in range(lines)]
        return jnp.concatenate(parts, axis=1).astype(I32)

    return row(0), row(lines)


def group(mine, theirs, face, live, sign, half, width):
    faces = face.shape[1]
    here = column_one_hot(mine, faces)
    gather = jnp.concatenate([here, column_one_hot(theirs, faces)], axis=0).T
    bit, low = cut(face, half)
    lines = jnp.concatenate([low, bit, jnp.zeros((6, faces), I32)], axis=0)
    ends = dot(lines.astype(F32).astype(BF), here).astype(I32)
    low, bit = ends[0:1, :], ends[1:2, :]
    ones = column_one_hot(jnp.where(live, low, -1), half)
    return gather, ones if sign > 0 else -ones, column_mask(bit, width)


def setup_kernel(
    tops_ref, etop_ref, ebot_ref, live_ref, nbr_ref, weights_ref, nodes_ref, raw_biases_ref,
    pick_ref, spread_ref, mask_ref, gather_ref, sum_ref, half_ref,
    ends_w_ref, hidden_ref, join_ref, out_w_ref, biases_ref,
):
    half = spread_ref.shape[0]
    width = mask_ref.shape[1]
    slots = etop_ref.shape[1]
    for d in range(2):
        live = lax.broadcasted_iota(I32, (1, slots), 1) < live_ref[0, d]
        gather_ref[d], sum_ref[d], half_ref[d] = group(
            etop_ref[d : d + 1, :], ebot_ref[d : d + 1, :], tops_ref[d : d + 1, :],
            live, 1, half, width,
        )
    rows = nbr_ref.shape[1]
    for k in range(nbr_ref.shape[0]):
        here = slice(k * rows, (k + 1) * rows)
        bit, low = cut(nbr_ref[k : k + 1, :], half)
        ones = column_one_hot(low, half)
        pick_ref[here, :] = ones.T
        spread_ref[:, here] = -ones
        mask_ref[here, :] = column_mask(bit, width)
    biases_ref[...] = raw_biases_ref[...] * 0.5
    zero = jnp.zeros((width, width), BF)
    for step in range(weights_ref.shape[0]):
        ends_w_ref[step, 0] = weights_ref[step, 0] * BF(0.5)
        ends_w_ref[step, 1] = weights_ref[step, 1] * BF(0.5)
        hidden = weights_ref[step, 2] * BF(0.5)
        hidden_ref[step] = jnp.concatenate(
            [jnp.concatenate([hidden, zero], axis=1), jnp.concatenate([zero, hidden], axis=1)],
            axis=0,
        )
        fold = dot(weights_ref[step, 3], nodes_ref[step, 1]).astype(BF)
        join_ref[step] = jnp.concatenate([nodes_ref[step, 0], fold], axis=0) * BF(0.5)
        out_w_ref[step] = nodes_ref[step, 2]


def inner_kernel(
    step, latent_ref, send_0, send_1, send_2, send_3, ends_w_ref, hidden_ref, biases_ref,
    pick_ref, spread_ref, mask_ref, total_ref, table_ref,
):
    rows, width = latent_ref.shape
    half = rows // 2
    faces = table_ref.shape[1]
    sends = (send_0, send_1, send_2, send_3)
    for d, odd in enumerate(odd_place()):
        near, far = (sends[PLACE[2 * d + i]][0:faces, :] for i in range(2))
        top, bottom = in_order(odd, near, far)
        table_ref[2 * d] = dot(top, ends_w_ref[step, 0]).astype(BF)
        table_ref[2 * d + 1] = dot(bottom, ends_w_ref[step, 1]).astype(BF)
    latent = latent_ref[...]
    source = dot(latent, ends_w_ref[step, 0]) + biases_ref[0, step : step + 1, :]
    table = halves(dot(latent, ends_w_ref[step, 1]).astype(BF))
    c1 = biases_ref[1, step : step + 1, :]
    c1 = jnp.concatenate([c1, c1], axis=1)
    fanout = pick_ref.shape[0] // rows
    total = None
    ended = None
    for pair in range(0, fanout, 2):
        here = [slice(k * rows, (k + 1) * rows) for k in (pair, pair + 1)]
        first = [
            half_silu(choose(dot(pick_ref[k, :], table), mask_ref[k, :]) + source).astype(BF)
            for k in here
        ]
        first = jnp.concatenate(first, axis=1)
        second = [
            half_silu(dot(first[a : a + CUT], hidden_ref[step]) + c1) for a in range(0, rows, CUT)
        ]
        started = jnp.concatenate([q[:, :width] + q[:, width:] for q in second], axis=0)
        total = started if total is None else total + started
        second = jnp.concatenate([q.astype(BF) for q in second], axis=0)
        values = [
            by_half(second[:, i * width : (i + 1) * width], mask_ref[k, :])
            for i, k in enumerate(here)
        ]
        part = jnp.concatenate(
            [dot(spread_ref[a : a + CUT, here[0]], values[0])
             + dot(spread_ref[a : a + CUT, here[1]], values[1]) for a in range(0, half, CUT)],
            axis=0,
        )
        ended = part if ended is None else ended + part
    total_ref[0:half, :] = total[0:half] + ended[:, :width]
    total_ref[half:, :] = total[half:] + ended[:, width:]


def cross(step, d, upper, lower, ends_w_ref, hidden_ref, biases_ref, table_ref, groups):
    width = upper.shape[1]
    c0 = biases_ref[0, step : step + 1, :]
    c1 = biases_ref[1, step : step + 1, :]
    c1 = jnp.concatenate([c1, c1], axis=1)
    far = (
        dot(upper, ends_w_ref[step, 1]).astype(BF),
        dot(lower, ends_w_ref[step, 0]).astype(BF),
    )
    first = []
    for i, (gather, _, _) in enumerate(groups):
        table = jnp.concatenate([table_ref[2 * d + i], far[i]], axis=0)
        first.append(half_silu(dot(gather, table) + c0).astype(BF))
    first = jnp.concatenate(first, axis=1)
    second = jnp.concatenate(
        [half_silu(dot(first[a : a + CUT], hidden_ref[step]) + c1).astype(BF)
         for a in range(0, first.shape[0], CUT)],
        axis=0,
    )
    values = [
        by_half(second[:, i * width : (i + 1) * width], mask)
        for i, (_, _, mask) in enumerate(groups)
    ]
    total = jnp.concatenate(
        [dot(groups[0][1][a : a + CUT], values[0]) + dot(groups[1][1][a : a + CUT], values[1])
         for a in range(0, groups[0][1].shape[0], CUT)],
        axis=0,
    )
    return total


def lower_group(ends, bottoms_ref, d, half):
    etop, ebot = unpacked(ends)
    return group(ebot, etop, bottoms_ref[d : d + 1, :], ebot >= 0, -1, half, ends.shape[1])


def along(step, d, refs, rows):
    near_ref, far_ref, ends_w_ref, hidden_ref, biases_ref, table_ref = refs[:6]
    own = tuple(ref[d] for ref in refs[6:9])
    half = rows // 2
    faces = table_ref.shape[1]
    upper, lower = in_order(odd_place()[d], near_ref[...], far_ref[...])
    if step == 0:
        bottoms_ref, keep = refs[9], refs[-3:]
        for ref, value in zip(keep, lower_group(lower[faces:], bottoms_ref, d, half)):
            ref[...] = value
        used = 10
    else:
        keep = refs[9:12]
        used = 12
    both = cross(
        step, d, upper[:faces], lower[:faces], ends_w_ref, hidden_ref, biases_ref, table_ref,
        (own, tuple(ref[...] for ref in keep)),
    )
    return both, used


def x_kernel(step, total_ref, *refs):
    rows, width = total_ref.shape
    half = rows // 2
    both, used = along(step, 0, refs, rows)
    out_ref = refs[used]
    out_ref[0:half, :] = total_ref[0:half, :] + both[:, :width]
    out_ref[half:, :] = total_ref[half:, :] + both[:, width:]


def y_kernel(step, last, total_ref, *refs):
    rows, width = total_ref.shape
    both, used = along(step, 1, refs, rows)
    biases_ref = refs[4]
    latent_ref, join_ref, out_w_ref = refs[used : used + 3]
    rest = refs[used + 3 :]
    arrived = total_ref[...] + jnp.concatenate([both[:, :width], both[:, width:]], axis=0)
    latent = latent_ref[...]
    joined = jnp.concatenate([latent, arrived.astype(BF)], axis=1)
    update = half_silu(dot(joined, join_ref[step]) + biases_ref[2, step : step + 1, :]).astype(BF)
    latent = (latent.astype(F32) + dot(update, out_w_ref[step])).astype(BF)
    if last:
        rest[0][...] = latent
    else:
        pick_ref, pick_mask_ref, out_ref = rest[:3]
        out_ref[...] = latent
        pick_faces(latent, pick_ref, pick_mask_ref, rest[3:7])


def local(
    latent,
    neighbours,
    top_rows,
    bottom_rows,
    edge_top,
    edge_bottom,
    live_count,
    edge_weights,
    node_weights,
    biases,
):
    latent_now = latent[0, 0]
    rows, width = latent_now.shape
    half = rows // 2
    nbr = neighbours[0, 0]
    tops = top_rows[0, 0]
    bottoms = bottom_rows[0, 0]
    etop = edge_top[0, 0]
    ebot = edge_bottom[0, 0]
    live = live_count.T
    bias_rows = jnp.swapaxes(biases, 0, 1)
    fanout = nbr.shape[0]
    faces = tops.shape[1]
    slots = etop.shape[1]
    steps = edge_weights.shape[0]
    like = jax.ShapeDtypeStruct
    face = like((faces, width), BF)
    lines = 2 * (slots // width)
    packed = like((faces + lines, width), BF)
    *sends, pick, pick_mask = call(
        first_kernel,
        [packed] * 4 + [like((4, faces, half), BF), like((4, faces, width), BF)],
        (latent_now, tops, bottoms, etop, ebot, live),
        in_specs=[HBM] * 6,
        scratch=[
            pltpu.VMEM((rows, width), BF), pltpu.VMEM(tops.shape, I32),
            pltpu.VMEM(tops.shape, I32), pltpu.VMEM(etop.shape, I32), pltpu.VMEM(etop.shape, I32),
            pltpu.SMEM(live.shape, I32), pltpu.SemaphoreType.DMA((6,)),
        ],
        name="first",
        grant=54 << 20,
    )
    group_like = [
        like((slots, 2 * faces), BF), like((half, slots), BF), like((slots, width), BF)
    ]
    kept_x = kept_y = None
    for step in range(steps):
        first, last = step == 0, step == steps - 1
        near_x, far_x, near_y, far_y = (sends[place] for place in PLACE)
        got_far_y = swapped(far_y, "gy", 1)
        got_near_y = swapped(near_y, "gy", 0)
        got_far_x = swapped(far_x, "gx", 1)
        got_near_x = swapped(near_x, "gx", 0)
        if first:
            made = call(
                setup_kernel,
                [like((fanout * rows, half), BF), like((half, fanout * rows), BF),
                 like((fanout * rows, width), BF)]
                + [like((2,) + g.shape, BF) for g in group_like]
                + [like((steps, 2, width, width), BF), like((steps, 2 * width, 2 * width), BF),
                   like((steps, 2 * width, width), BF), like((steps, width, width), BF),
                   like(bias_rows.shape, F32)],
                (tops, etop, ebot, live, nbr, edge_weights, node_weights, bias_rows),
                in_specs=[VMEM] * 3 + [SMEM] + [VMEM] * 4,
                name="setup",
            )
            inner, own = made[:3], made[3:6]
            ends_w, hidden, join, out_w, half_biases = made[6:]
            edge_net = (ends_w, hidden, half_biases)
        total, table = call(
            functools.partial(inner_kernel, step),
            [like((rows, width), F32), like((4, faces, width), BF)],
            (latent_now, *sends, *edge_net, *inner),
            name="inner",
        )
        total, *made = call(
            functools.partial(x_kernel, step),
            [like((rows, width), F32)] + (group_like if first else []),
            (total, got_near_x, got_far_x, *edge_net, table, *own,
             *([bottoms] if first else kept_x)),
            name="along_x",
        )
        kept_x = made if first else kept_x
        latent_now, *made = call(
            functools.partial(y_kernel, step, last),
            [like((rows, width), BF)] + ([] if last else [face] * 4)
            + (group_like if first else []),
            (total, got_near_y, got_far_y, *edge_net, table, *own,
             *([bottoms] if first else kept_y), latent_now, join, out_w,
             *([] if last else [pick, pick_mask])),
            name="along_y",
        )
        sends, made = made[:4], made[4:]
        kept_y = made if first else kept_y
    return latent_now[None, None]


def solution(mesh):
    return jax.shard_map(
        local,
        mesh=mesh,
        in_specs=(
            P("gx", "gy", None, None),
            P("gx", "gy", None, None),
            P("gx", "gy", None, None),
            P("gx", "gy", None, None),
            P("gx", "gy", None, None),
            P("gx", "gy", None, None),
            P(None, ("gx", "gy")),
            P(),
            P(),
            P(),
        ),
        out_specs=P("gx", "gy", None, None),
        check_vma=False,
    )
```

```python
import functools

import jax
import jax.numpy as jnp
from jax import lax
from jax.experimental import pallas as pl
from jax.experimental.pallas import tpu as pltpu
from jax.sharding import PartitionSpec as P

BF = jnp.bfloat16
F32 = jnp.float32
I32 = jnp.int32
VMEM = pl.BlockSpec(memory_space=pltpu.VMEM)
SMEM = pl.BlockSpec(memory_space=pltpu.SMEM)
HBM = pl.BlockSpec(memory_space=pltpu.HBM)

CUT = 128
AHEAD = F32

NEAR_X, FAR_X, NEAR_Y, FAR_Y = range(4)
ORDER = (FAR_Y, FAR_X, NEAR_Y, NEAR_X)
PLACE = tuple(ORDER.index(link) for link in range(4))


def swapped(block, axis, odd):
    count = lax.axis_size(axis)
    route = []
    for i in range(odd, count, 2):
        j = (i + 1) % count
        route += [(i, j), (j, i)]
    return lax.ppermute(block, axis, route)


def call(kernel, outs, operands, in_specs=None, scratch=(), name=None, grant=40 << 20):
    moved = sum(o.size * o.dtype.itemsize for o in operands)
    return pl.pallas_call(
        kernel,
        out_shape=outs,
        in_specs=in_specs or [VMEM] * len(operands),
        out_specs=[VMEM] * len(outs),
        scratch_shapes=list(scratch),
        compiler_params=pltpu.CompilerParams(vmem_limit_bytes=grant),
        cost_estimate=pl.CostEstimate(flops=1 << 30, bytes_accessed=moved, transcendentals=0),
        name=name,
    )(*operands)


def dot(a, b):
    return jnp.dot(a, b, preferred_element_type=F32)


def half_silu(y):
    return y + y * jnp.tanh(y)


def column_one_hot(row, depth):
    depths = lax.broadcasted_iota(jnp.int16, (depth, row.shape[1]), 0)
    return jnp.where(depths == row.astype(jnp.int16), BF(1), BF(0))


def column_mask(bit, width):
    return jnp.broadcast_to(bit.astype(F32).astype(BF), (width, bit.shape[1])).T


def cut(row, half):
    bit = (row >= half).astype(I32)
    return bit, row - bit * half


def halves(table):
    half = table.shape[0] // 2
    return jnp.concatenate([table[:half], table[half:]], axis=1)


def choose(both, mask):
    width = both.shape[1] // 2
    return jnp.where(mask > 0, both[:, width:], both[:, :width])


def by_half(values, mask):
    upper = values * mask
    return jnp.concatenate([values - upper, upper], axis=1)


def odd_place():
    return lax.axis_index("gx") % 2, lax.axis_index("gy") % 2


def in_order(odd, first, second):
    turned = odd == 1
    return jnp.where(turned, second, first), jnp.where(turned, first, second)


def pick_faces(latent, pick_ref, pick_mask_ref, out_refs):
    table = halves(latent)
    rows = [
        choose(dot(pick_ref[face], table), pick_mask_ref[face]).astype(BF) for face in range(4)
    ]
    for d, odd in enumerate(odd_place()):
        near, far = in_order(odd, rows[2 * d], rows[2 * d + 1])
        count = near.shape[0]
        out_refs[PLACE[2 * d]][0:count, :] = near
        out_refs[PLACE[2 * d + 1]][0:count, :] = far


def first_kernel(
    latent_hbm, tops_hbm, bottoms_hbm, etop_hbm, ebot_hbm, live_hbm,
    send_0, send_1, send_2, send_3, pick_ref, pick_mask_ref,
    latent_ref, tops_ref, bottoms_ref, etop_ref, ebot_ref, live_ref, sems,
):
    moves = [
        pltpu.make_async_copy(src, dst, sems.at[i])
        for i, (src, dst) in enumerate((
            (tops_hbm, tops_ref), (bottoms_hbm, bottoms_ref), (latent_hbm, latent_ref),
            (etop_hbm, etop_ref), (ebot_hbm, ebot_ref), (live_hbm, live_ref),
        ))
    ]
    for move in moves:
        move.start()
    half = latent_ref.shape[0] // 2
    width = latent_ref.shape[1]
    moves[0].wait()
    moves[1].wait()
    for face in range(4):
        d, ref = face // 2, (tops_ref, bottoms_ref)[face % 2]
        bit, low = cut(ref[d : d + 1, :], half)
        pick_ref[face] = column_one_hot(low, half).T
        pick_mask_ref[face] = column_mask(bit, width)
    for move in moves[2:]:
        move.wait()
    sends = (send_0, send_1, send_2, send_3)
    pick_faces(latent_ref[...], pick_ref, pick_mask_ref, sends)
    faces = tops_ref.shape[1]
    slots = etop_ref.shape[1]
    lines = slots // width
    for d in range(2):
        live = lax.broadcasted_iota(I32, (1, slots), 1) < live_ref[0, d]
        etop = etop_ref[d : d + 1, :].astype(F32)
        ebot = jnp.where(live, ebot_ref[d : d + 1, :], -1).astype(F32)
        rows = [v[:, i * width : (i + 1) * width] for v in (etop, ebot) for i in range(lines)]
        ends = jnp.concatenate(rows, axis=0).astype(BF)
        sends[PLACE[2 * d]][faces:, :] = ends
        sends[PLACE[2 * d + 1]][faces:, :] = ends


def unpacked(ends):
    ends = ends.astype(F32)
    lines = ends.shape[0] // 2

    def row(start):
        parts = [ends[start + i : start + i + 1, :] for i in range(lines)]
        return jnp.concatenate(parts, axis=1).astype(I32)

    return row(0), row(lines)


def group(mine, theirs, face, live, sign, half, width):
    faces = face.shape[1]
    here = column_one_hot(mine, faces)
    gather = jnp.concatenate([here, column_one_hot(theirs, faces)], axis=0).T
    bit, low = cut(face, half)
    lines = jnp.concatenate([low, bit, jnp.zeros((6, faces), I32)], axis=0)
    ends = dot(lines.astype(F32).astype(BF), here).astype(I32)
    low, bit = ends[0:1, :], ends[1:2, :]
    ones = column_one_hot(jnp.where(live, low, -1), half)
    return gather, ones if sign > 0 else -ones, column_mask(bit, width)


def setup_kernel(
    tops_ref, etop_ref, ebot_ref, live_ref, nbr_ref, weights_ref, nodes_ref, raw_biases_ref,
    pick_ref, spread_ref, mask_ref, gather_ref, sum_ref, half_ref,
    ends_w_ref, hidden_ref, join_ref, out_w_ref, biases_ref,
):
    half = spread_ref.shape[0]
    width = mask_ref.shape[1]
    slots = etop_ref.shape[1]
    for d in range(2):
        live = lax.broadcasted_iota(I32, (1, slots), 1) < live_ref[0, d]
        gather_ref[d], sum_ref[d], half_ref[d] = group(
            etop_ref[d : d + 1, :], ebot_ref[d : d + 1, :], tops_ref[d : d + 1, :],
            live, 1, half, width,
        )
    rows = nbr_ref.shape[1]
    for k in range(nbr_ref.shape[0]):
        here = slice(k * rows, (k + 1) * rows)
        bit, low = cut(nbr_ref[k : k + 1, :], half)
        ones = column_one_hot(low, half)
        pick_ref[here, :] = ones.T
        spread_ref[:, here] = -ones
        mask_ref[here, :] = column_mask(bit, width)
    biases_ref[...] = raw_biases_ref[...] * 0.5
    zero = jnp.zeros((width, width), BF)
    for step in range(weights_ref.shape[0]):
        ends_w_ref[step, 0] = weights_ref[step, 0] * BF(0.5)
        ends_w_ref[step, 1] = weights_ref[step, 1] * BF(0.5)
        hidden = weights_ref[step, 2] * BF(0.5)
        hidden_ref[step] = jnp.concatenate(
            [jnp.concatenate([hidden, zero], axis=1), jnp.concatenate([zero, hidden], axis=1)],
            axis=0,
        )
        fold = dot(weights_ref[step, 3], nodes_ref[step, 1]).astype(BF)
        join_ref[step] = jnp.concatenate([nodes_ref[step, 0], fold], axis=0) * BF(0.5)
        out_w_ref[step] = nodes_ref[step, 2]


def inner_kernel(
    step, latent_ref, send_0, send_1, send_2, send_3, ends_w_ref, hidden_ref, biases_ref,
    pick_ref, spread_ref, mask_ref, *refs,
):
    if step > 0:
        own_gather_ref, lower_x_ref, lower_y_ref, total_ref, table_ref, ahead_ref = refs
    else:
        total_ref, table_ref = refs
    rows, width = latent_ref.shape
    half = rows // 2
    faces = table_ref.shape[1]
    sends = (send_0, send_1, send_2, send_3)
    for d, odd in enumerate(odd_place()):
        near, far = (sends[PLACE[2 * d + i]][0:faces, :] for i in range(2))
        top, bottom = in_order(odd, near, far)
        table_ref[2 * d] = dot(top, ends_w_ref[step, 0]).astype(BF)
        table_ref[2 * d + 1] = dot(bottom, ends_w_ref[step, 1]).astype(BF)
    latent = latent_ref[...]
    source = dot(latent, ends_w_ref[step, 0]) + biases_ref[0, step : step + 1, :]
    table = halves(dot(latent, ends_w_ref[step, 1]).astype(BF))
    c1 = biases_ref[1, step : step + 1, :]
    c1 = jnp.concatenate([c1, c1], axis=1)
    fanout = pick_ref.shape[0] // rows
    total = None
    ended = None
    for pair in range(0, fanout, 2):
        here = [slice(k * rows, (k + 1) * rows) for k in (pair, pair + 1)]
        first = [
            half_silu(choose(dot(pick_ref[k, :], table), mask_ref[k, :]) + source).astype(BF)
            for k in here
        ]
        first = jnp.concatenate(first, axis=1)
        second = [
            half_silu(dot(first[a : a + CUT], hidden_ref[step]) + c1) for a in range(0, rows, CUT)
        ]
        started = jnp.concatenate([q[:, :width] + q[:, width:] for q in second], axis=0)
        total = started if total is None else total + started
        second = jnp.concatenate([q.astype(BF) for q in second], axis=0)
        values = [
            by_half(second[:, i * width : (i + 1) * width], mask_ref[k, :])
            for i, k in enumerate(here)
        ]
        part = jnp.concatenate(
            [dot(spread_ref[a : a + CUT, here[0]], values[0])
             + dot(spread_ref[a : a + CUT, here[1]], values[1]) for a in range(0, half, CUT)],
            axis=0,
        )
        ended = part if ended is None else ended + part
    total_ref[0:half, :] = total[0:half] + ended[:, :width]
    total_ref[half:, :] = total[half:] + ended[:, width:]
    if step > 0:
        c0 = biases_ref[0, step : step + 1, :]
        for d, lower_ref in enumerate((lower_x_ref, lower_y_ref)):
            for i, gather in enumerate((own_gather_ref[d], lower_ref[...])):
                link = 2 * d + i
                ahead_ref[link] = (dot(gather[:, :faces], table_ref[link]) + c0).astype(ahead_ref.dtype)


def cross(step, d, upper, lower, ends_w_ref, hidden_ref, biases_ref, table_ref, ahead_ref, groups):
    width = upper.shape[1]
    c0 = biases_ref[0, step : step + 1, :]
    c1 = biases_ref[1, step : step + 1, :]
    c1 = jnp.concatenate([c1, c1], axis=1)
    far = (
        dot(upper, ends_w_ref[step, 1]).astype(BF),
        dot(lower, ends_w_ref[step, 0]).astype(BF),
    )
    first = []
    for i, (gather, _, _) in enumerate(groups):
        if step > 0:
            faces = far[i].shape[0]
            y = dot(gather[:, faces:], far[i]) + ahead_ref[2 * d + i]
        else:
            table = jnp.concatenate([table_ref[2 * d + i], far[i]], axis=0)
            y = dot(gather, table) + c0
        first.append(half_silu(y).astype(BF))
    first = jnp.concatenate(first, axis=1)
    second = jnp.concatenate(
        [half_silu(dot(first[a : a + CUT], hidden_ref[step]) + c1).astype(BF)
         for a in range(0, first.shape[0], CUT)],
        axis=0,
    )
    values = [
        by_half(second[:, i * width : (i + 1) * width], mask)
        for i, (_, _, mask) in enumerate(groups)
    ]
    total = jnp.concatenate(
        [dot(groups[0][1][a : a + CUT], values[0]) + dot(groups[1][1][a : a + CUT], values[1])
         for a in range(0, groups[0][1].shape[0], CUT)],
        axis=0,
    )
    return total


def lower_group(ends, bottoms_ref, d, half):
    etop, ebot = unpacked(ends)
    return group(ebot, etop, bottoms_ref[d : d + 1, :], ebot >= 0, -1, half, ends.shape[1])


def along(step, d, refs, rows):
    near_ref, far_ref, ends_w_ref, hidden_ref, biases_ref, table_ref = refs[:6]
    ahead_ref = None
    if step > 0:
        ahead_ref, refs = refs[6], refs[:6] + refs[7:]
    own = tuple(ref[d] for ref in refs[6:9])
    half = rows // 2
    faces = table_ref.shape[1]
    upper, lower = in_order(odd_place()[d], near_ref[...], far_ref[...])
    if step == 0:
        bottoms_ref, keep = refs[9], refs[-3:]
        for ref, value in zip(keep, lower_group(lower[faces:], bottoms_ref, d, half)):
            ref[...] = value
        used = 10
    else:
        keep = refs[9:12]
        used = 12
    both = cross(
        step, d, upper[:faces], lower[:faces], ends_w_ref, hidden_ref, biases_ref, table_ref,
        ahead_ref, (own, tuple(ref[...] for ref in keep)),
    )
    return both, used + (step > 0)


def x_kernel(step, total_ref, *refs):
    rows, width = total_ref.shape
    half = rows // 2
    both, used = along(step, 0, refs, rows)
    out_ref = refs[used]
    out_ref[0:half, :] = total_ref[0:half, :] + both[:, :width]
    out_ref[half:, :] = total_ref[half:, :] + both[:, width:]


def y_kernel(step, last, total_ref, *refs):
    rows, width = total_ref.shape
    both, used = along(step, 1, refs, rows)
    biases_ref = refs[4]
    latent_ref, join_ref, out_w_ref = refs[used : used + 3]
    rest = refs[used + 3 :]
    arrived = total_ref[...] + jnp.concatenate([both[:, :width], both[:, width:]], axis=0)
    latent = latent_ref[...]
    joined = jnp.concatenate([latent, arrived.astype(BF)], axis=1)
    update = half_silu(dot(joined, join_ref[step]) + biases_ref[2, step : step + 1, :]).astype(BF)
    latent = (latent.astype(F32) + dot(update, out_w_ref[step])).astype(BF)
    if last:
        rest[0][...] = latent
    else:
        pick_ref, pick_mask_ref, out_ref = rest[:3]
        out_ref[...] = latent
        pick_faces(latent, pick_ref, pick_mask_ref, rest[3:7])


def local(
    latent,
    neighbours,
    top_rows,
    bottom_rows,
    edge_top,
    edge_bottom,
    live_count,
    edge_weights,
    node_weights,
    biases,
):
    latent_now = latent[0, 0]
    rows, width = latent_now.shape
    half = rows // 2
    nbr = neighbours[0, 0]
    tops = top_rows[0, 0]
    bottoms = bottom_rows[0, 0]
    etop = edge_top[0, 0]
    ebot = edge_bottom[0, 0]
    live = live_count.T
    bias_rows = jnp.swapaxes(biases, 0, 1)
    fanout = nbr.shape[0]
    faces = tops.shape[1]
    slots = etop.shape[1]
    steps = edge_weights.shape[0]
    like = jax.ShapeDtypeStruct
    face = like((faces, width), BF)
    lines = 2 * (slots // width)
    packed = like((faces + lines, width), BF)
    *sends, pick, pick_mask = call(
        first_kernel,
        [packed] * 4 + [like((4, faces, half), BF), like((4, faces, width), BF)],
        (latent_now, tops, bottoms, etop, ebot, live),
        in_specs=[HBM] * 6,
        scratch=[
            pltpu.VMEM((rows, width), BF), pltpu.VMEM(tops.shape, I32),
            pltpu.VMEM(tops.shape, I32), pltpu.VMEM(etop.shape, I32), pltpu.VMEM(etop.shape, I32),
            pltpu.SMEM(live.shape, I32), pltpu.SemaphoreType.DMA((6,)),
        ],
        name="first",
        grant=54 << 20,
    )
    group_like = [
        like((slots, 2 * faces), BF), like((half, slots), BF), like((slots, width), BF)
    ]
    kept_x = kept_y = None
    for step in range(steps):
        first, last = step == 0, step == steps - 1
        near_x, far_x, near_y, far_y = (sends[place] for place in PLACE)
        got_far_y = swapped(far_y, "gy", 1)
        got_near_y = swapped(near_y, "gy", 0)
        got_far_x = swapped(far_x, "gx", 1)
        got_near_x = swapped(near_x, "gx", 0)
        if first:
            made = call(
                setup_kernel,
                [like((fanout * rows, half), BF), like((half, fanout * rows), BF),
                 like((fanout * rows, width), BF)]
                + [like((2,) + g.shape, BF) for g in group_like]
                + [like((steps, 2, width, width), BF), like((steps, 2 * width, 2 * width), BF),
                   like((steps, 2 * width, width), BF), like((steps, width, width), BF),
                   like(bias_rows.shape, F32)],
                (tops, etop, ebot, live, nbr, edge_weights, node_weights, bias_rows),
                in_specs=[VMEM] * 3 + [SMEM] + [VMEM] * 4,
                name="setup",
            )
            inner, own = made[:3], made[3:6]
            ends_w, hidden, join, out_w, half_biases = made[6:]
            edge_net = (ends_w, hidden, half_biases)
        gathers = () if first else (own[0], kept_x[0], kept_y[0])
        total, *tables = call(
            functools.partial(inner_kernel, step),
            [like((rows, width), F32), like((4, faces, width), BF)]
            + ([] if first else [like((4, slots, width), AHEAD)]),
            (latent_now, *sends, *edge_net, *inner, *gathers),
            name="inner",
        )
        total, *made = call(
            functools.partial(x_kernel, step),
            [like((rows, width), F32)] + (group_like if first else []),
            (total, got_near_x, got_far_x, *edge_net, *tables, *own,
             *([bottoms] if first else kept_x)),
            name="along_x",
        )
        kept_x = made if first else kept_x
        latent_now, *made = call(
            functools.partial(y_kernel, step, last),
            [like((rows, width), BF)] + ([] if last else [face] * 4)
            + (group_like if first else []),
            (total, got_near_y, got_far_y, *edge_net, *tables, *own,
             *([bottoms] if first else kept_y), latent_now, join, out_w,
             *([] if last else [pick, pick_mask])),
            name="along_y",
        )
        sends, made = made[:4], made[4:]
        kept_y = made if first else kept_y
    return latent_now[None, None]


def solution(mesh):
    return jax.shard_map(
        local,
        mesh=mesh,
        in_specs=(
            P("gx", "gy", None, None),
            P("gx", "gy", None, None),
            P("gx", "gy", None, None),
            P("gx", "gy", None, None),
            P("gx", "gy", None, None),
            P("gx", "gy", None, None),
            P(None, ("gx", "gy")),
            P(),
            P(),
            P(),
        ),
        out_specs=P("gx", "gy", None, None),
        check_vma=False,
    )
```

```python
import functools

import jax
import jax.numpy as jnp
from jax import lax
from jax.experimental import pallas as pl
from jax.experimental.pallas import tpu as pltpu
from jax.sharding import PartitionSpec as P

BF = jnp.bfloat16
F32 = jnp.float32
I32 = jnp.int32
VMEM = pl.BlockSpec(memory_space=pltpu.VMEM)
HBM = pl.BlockSpec(memory_space=pltpu.HBM)

CUT = 128

NEAR_X, FAR_X, NEAR_Y, FAR_Y = range(4)
ORDER = (FAR_Y, FAR_X, NEAR_Y, NEAR_X)
VISITS = ((NEAR_X, FAR_Y), (FAR_X, NEAR_Y))
PLACE = tuple(ORDER.index(link) for link in range(4))


def swapped(block, axis, odd):
    count = lax.axis_size(axis)
    route = []
    for i in range(odd, count, 2):
        j = (i + 1) % count
        route += [(i, j), (j, i)]
    return lax.ppermute(block, axis, route)


def call(kernel, outs, operands, in_specs=None, scratch=(), name=None, grant=40 << 20):
    moved = sum(o.size * o.dtype.itemsize for o in operands)
    return pl.pallas_call(
        kernel,
        out_shape=outs,
        in_specs=in_specs or [VMEM] * len(operands),
        out_specs=[VMEM] * len(outs),
        scratch_shapes=list(scratch),
        compiler_params=pltpu.CompilerParams(vmem_limit_bytes=grant),
        cost_estimate=pl.CostEstimate(flops=1 << 30, bytes_accessed=moved, transcendentals=0),
        name=name,
    )(*operands)


def dot(a, b):
    return jnp.dot(a, b, preferred_element_type=F32)


def half_silu(y):
    return y + y * jnp.tanh(y)


def column_one_hot(row, depth):
    depths = lax.broadcasted_iota(jnp.int16, (depth, row.shape[1]), 0)
    return jnp.where(depths == row.astype(jnp.int16), BF(1), BF(0))


def column_mask(bit, width):
    return jnp.broadcast_to(bit.astype(F32).astype(BF), (width, bit.shape[1])).T


def cut(row, half):
    bit = (row >= half).astype(I32)
    return bit, row - bit * half


def halves(table):
    half = table.shape[0] // 2
    return jnp.concatenate([table[:half], table[half:]], axis=1)


def choose(both, mask):
    width = both.shape[1] // 2
    return jnp.where(mask > 0, both[:, width:], both[:, :width])


def by_half(values, mask):
    upper = values * mask
    return jnp.concatenate([values - upper, upper], axis=1)


def odd_place():
    return lax.axis_index("gx") % 2, lax.axis_index("gy") % 2


def role_of(link):
    return (odd_place()[link // 2] + link % 2) % 2


def in_order(odd, first, second):
    turned = odd == 1
    return jnp.where(turned, second, first), jnp.where(turned, first, second)


def pick_faces(latent, pick_ref, pick_mask_ref, out_refs):
    table = halves(latent)
    rows = [
        choose(dot(pick_ref[face], table), pick_mask_ref[face]).astype(BF) for face in range(4)
    ]
    for d, odd in enumerate(odd_place()):
        near, far = in_order(odd, rows[2 * d], rows[2 * d + 1])
        count = near.shape[0]
        out_refs[PLACE[2 * d]][0:count, :] = near
        out_refs[PLACE[2 * d + 1]][0:count, :] = far


def first_kernel(
    latent_hbm, tops_hbm, bottoms_hbm, etop_hbm, ebot_hbm, live_hbm,
    send_0, send_1, send_2, send_3, pick_ref, pick_mask_ref, ends_ref,
    latent_ref, tops_ref, bottoms_ref, etop_ref, ebot_ref, live_ref, sems,
):
    moves = [
        pltpu.make_async_copy(src, dst, sems.at[i])
        for i, (src, dst) in enumerate((
            (tops_hbm, tops_ref), (bottoms_hbm, bottoms_ref), (latent_hbm, latent_ref),
            (etop_hbm, etop_ref), (ebot_hbm, ebot_ref), (live_hbm, live_ref),
        ))
    ]
    for move in moves:
        move.start()
    half = latent_ref.shape[0] // 2
    width = latent_ref.shape[1]
    moves[0].wait()
    moves[1].wait()
    for face in range(4):
        d, ref = face // 2, (tops_ref, bottoms_ref)[face % 2]
        bit, low = cut(ref[d : d + 1, :], half)
        pick_ref[face] = column_one_hot(low, half).T
        pick_mask_ref[face] = column_mask(bit, width)
    for move in moves[2:]:
        move.wait()
    sends = (send_0, send_1, send_2, send_3)
    pick_faces(latent_ref[...], pick_ref, pick_mask_ref, sends)
    faces = tops_ref.shape[1]
    slots = etop_ref.shape[1]
    lines = slots // width
    for d in range(2):
        live = lax.broadcasted_iota(I32, (1, slots), 1) < live_ref[0, d]
        etop = etop_ref[d : d + 1, :].astype(F32)
        ebot = jnp.where(live, ebot_ref[d : d + 1, :], -1).astype(F32)
        rows = [v[:, i * width : (i + 1) * width] for v in (etop, ebot) for i in range(lines)]
        ends = jnp.concatenate(rows, axis=0).astype(BF)
        ends_ref[d] = ends
        sends[PLACE[2 * d]][faces:, :] = ends
        sends[PLACE[2 * d + 1]][faces:, :] = ends


def unpacked(ends):
    ends = ends.astype(F32)
    lines = ends.shape[0] // 2

    def row(start):
        parts = [ends[start + i : start + i + 1, :] for i in range(lines)]
        return jnp.concatenate(parts, axis=1).astype(I32)

    return row(0), row(lines)


def link_group(link, got_ref, ends_ref, tops_ref, bottoms_ref, half):
    d = link // 2
    owned = role_of(link) == 0
    faces = tops_ref.shape[1]
    width = got_ref.shape[1]
    etop, ebot = unpacked(jnp.where(owned, ends_ref[d], got_ref[faces:, :]))
    face = jnp.where(owned, tops_ref[d : d + 1, :], bottoms_ref[d : d + 1, :])
    here = column_one_hot(jnp.where(owned, etop, ebot), faces)
    there = column_one_hot(jnp.where(owned, ebot, etop), faces)
    bit, low = cut(face, half)
    lines = jnp.concatenate([low, bit, jnp.zeros((6, faces), I32)], axis=0)
    rows = dot(lines.astype(F32).astype(BF), here).astype(I32)
    low, bit = rows[0:1, :], rows[1:2, :]
    ones = column_one_hot(jnp.where(ebot >= 0, low, -1), half)
    gather = jnp.concatenate([here, there], axis=0).T
    return gather, jnp.where(owned, ones, -ones), column_mask(bit, width)


def link_first(step, link, got_ref, gather, ends_w_ref, biases_ref, table_ref, ahead_ref):
    role = role_of(link)
    faces = table_ref.shape[1]
    far = dot(got_ref[0:faces, :], ends_w_ref[step, 1 - role]).astype(BF)
    if step > 0:
        y = dot(gather[:, faces:], far) + ahead_ref[link]
    else:
        table = jnp.concatenate([table_ref[link], far], axis=0)
        y = dot(gather, table) + biases_ref[0, step : step + 1, :]
    return half_silu(y).astype(BF)


def second_layer(first, weight, bias):
    parts = [
        half_silu(dot(first[a : a + CUT], weight) + bias).astype(BF)
        for a in range(0, first.shape[0], CUT)
    ]
    return jnp.concatenate(parts, axis=0)


def placed(places, values):
    parts = []
    for a in range(0, places[0].shape[0], CUT):
        part = None
        for place, value in zip(places, values):
            product = dot(place[a : a + CUT], value)
            part = product if part is None else part + product
        parts.append(part)
    return jnp.concatenate(parts, axis=0)


def link_sums(step, links, gots, groups, ends_w_ref, hidden_ref, biases_ref, table_ref, ahead_ref):
    width = ends_w_ref.shape[2]
    wide = width * len(links)
    first = [
        link_first(step, link, got, group[0], ends_w_ref, biases_ref, table_ref, ahead_ref)
        for link, got, group in zip(links, gots, groups)
    ]
    bias = biases_ref[1, step : step + 1, :]
    second = second_layer(
        jnp.concatenate(first, axis=1),
        hidden_ref[step, 0:wide, 0:wide],
        jnp.concatenate([bias] * len(links), axis=1),
    )
    values = [
        by_half(second[:, i * width : (i + 1) * width], group[2]) for i, group in enumerate(groups)
    ]
    return placed([group[1] for group in groups], values)


def prepared(step, links, got_refs, refs, half):
    count = 3 * len(links)
    if step > 0:
        kept, rest = refs[:count], refs[count:]
    else:
        kept, rest = refs[-count:], refs[3:-count]
        for i, (link, got_ref) in enumerate(zip(links, got_refs)):
            for ref, value in zip(kept[3 * i :], link_group(link, got_ref, *refs[:3], half)):
                ref[...] = value
    return [tuple(ref[...] for ref in kept[i : i + 3]) for i in range(0, count, 3)], rest


def setup_kernel(
    nbr_ref, weights_ref, nodes_ref, raw_biases_ref,
    pick_ref, spread_ref, mask_ref, ends_w_ref, hidden_ref, join_ref, out_w_ref, biases_ref,
):
    half = spread_ref.shape[0]
    width = mask_ref.shape[1]
    rows = nbr_ref.shape[1]
    for k in range(nbr_ref.shape[0]):
        here = slice(k * rows, (k + 1) * rows)
        bit, low = cut(nbr_ref[k : k + 1, :], half)
        ones = column_one_hot(low, half)
        pick_ref[here, :] = ones.T
        spread_ref[:, here] = -ones
        mask_ref[here, :] = column_mask(bit, width)
    biases_ref[...] = raw_biases_ref[...] * 0.5
    zero = jnp.zeros((width, width), BF)
    for step in range(weights_ref.shape[0]):
        ends_w_ref[step, 0] = weights_ref[step, 0] * BF(0.5)
        ends_w_ref[step, 1] = weights_ref[step, 1] * BF(0.5)
        hidden = weights_ref[step, 2] * BF(0.5)
        hidden_ref[step] = jnp.concatenate(
            [jnp.concatenate([hidden, zero], axis=1), jnp.concatenate([zero, hidden], axis=1)],
            axis=0,
        )
        fold = dot(weights_ref[step, 3], nodes_ref[step, 1]).astype(BF)
        join_ref[step] = jnp.concatenate([nodes_ref[step, 0], fold], axis=0) * BF(0.5)
        out_w_ref[step] = nodes_ref[step, 2]


def inner_kernel(
    step, latent_ref, send_0, send_1, send_2, send_3, ends_w_ref, hidden_ref, biases_ref,
    pick_ref, spread_ref, mask_ref, *refs,
):
    rows, width = latent_ref.shape
    half = rows // 2
    sends = (send_0, send_1, send_2, send_3)
    if step > 0:
        gather_refs, (total_ref, table_ref, ahead_ref) = refs[:4], refs[4:]
    else:
        total_ref, table_ref = refs
    faces = table_ref.shape[1]
    for link in range(4):
        face = sends[PLACE[link]][0:faces, :]
        table_ref[link] = dot(face, ends_w_ref[step, role_of(link)]).astype(BF)
    latent = latent_ref[...]
    source = dot(latent, ends_w_ref[step, 0]) + biases_ref[0, step : step + 1, :]
    table = halves(dot(latent, ends_w_ref[step, 1]).astype(BF))
    c1 = biases_ref[1, step : step + 1, :]
    c1 = jnp.concatenate([c1, c1], axis=1)
    fanout = pick_ref.shape[0] // rows
    total = None
    ended = None
    for pair in range(0, fanout, 2):
        here = [slice(k * rows, (k + 1) * rows) for k in (pair, pair + 1)]
        first = [
            half_silu(choose(dot(pick_ref[k, :], table), mask_ref[k, :]) + source).astype(BF)
            for k in here
        ]
        first = jnp.concatenate(first, axis=1)
        second = [
            half_silu(dot(first[a : a + CUT], hidden_ref[step]) + c1) for a in range(0, rows, CUT)
        ]
        started = jnp.concatenate([q[:, :width] + q[:, width:] for q in second], axis=0)
        total = started if total is None else total + started
        second = jnp.concatenate([q.astype(BF) for q in second], axis=0)
        values = [
            by_half(second[:, i * width : (i + 1) * width], mask_ref[k, :])
            for i, k in enumerate(here)
        ]
        part = jnp.concatenate(
            [dot(spread_ref[a : a + CUT, here[0]], values[0])
             + dot(spread_ref[a : a + CUT, here[1]], values[1]) for a in range(0, half, CUT)],
            axis=0,
        )
        ended = part if ended is None else ended + part
    total_ref[0:half, :] = total[0:half] + ended[:, :width]
    total_ref[half:, :] = total[half:] + ended[:, width:]
    if step > 0:
        c0 = biases_ref[0, step : step + 1, :]
        for link, ref in enumerate(gather_refs):
            ahead_ref[link] = dot(ref[:, 0:faces], table_ref[link]) + c0


def cross_kernel(step, links, total_ref, *refs):
    rows, width = total_ref.shape
    half = rows // 2
    gots, refs = refs[: len(links)], refs[len(links) :]
    nets, refs = refs[: 4 + (step > 0)], refs[4 + (step > 0) :]
    groups, (out_ref,) = prepared(step, links, gots, refs, half)
    ahead_ref = nets[4] if step > 0 else None
    both = link_sums(step, links, gots, groups, *nets[:4], ahead_ref)
    out_ref[0:half, :] = total_ref[0:half, :] + both[:, :width]
    out_ref[half:, :] = total_ref[half:, :] + both[:, width:]


def last_kernel(step, links, last, total_ref, *refs):
    rows, width = total_ref.shape
    half = rows // 2
    gots, refs = refs[: len(links)], refs[len(links) :]
    nets, refs = refs[: 4 + (step > 0)], refs[4 + (step > 0) :]
    (latent_ref, join_ref, out_w_ref), refs = refs[:3], refs[3:]
    groups, rest = prepared(step, links, gots, refs, half)
    ahead_ref = nets[4] if step > 0 else None
    biases_ref = nets[2]
    both = link_sums(step, links, gots, groups, *nets[:4], ahead_ref)
    arrived = total_ref[...] + jnp.concatenate([both[:, :width], both[:, width:]], axis=0)
    latent = latent_ref[...]
    joined = jnp.concatenate([latent, arrived.astype(BF)], axis=1)
    update = half_silu(dot(joined, join_ref[step]) + biases_ref[2, step : step + 1, :]).astype(BF)
    latent = (latent.astype(F32) + dot(update, out_w_ref[step])).astype(BF)
    if last:
        rest[0][...] = latent
    else:
        pick_ref, pick_mask_ref, out_ref = rest[:3]
        out_ref[...] = latent
        pick_faces(latent, pick_ref, pick_mask_ref, rest[3:7])


def local(
    latent,
    neighbours,
    top_rows,
    bottom_rows,
    edge_top,
    edge_bottom,
    live_count,
    edge_weights,
    node_weights,
    biases,
):
    latent_now = latent[0, 0]
    rows, width = latent_now.shape
    half = rows // 2
    nbr = neighbours[0, 0]
    tops = top_rows[0, 0]
    bottoms = bottom_rows[0, 0]
    etop = edge_top[0, 0]
    ebot = edge_bottom[0, 0]
    live = live_count.T
    bias_rows = jnp.swapaxes(biases, 0, 1)
    fanout = nbr.shape[0]
    faces = tops.shape[1]
    slots = etop.shape[1]
    steps = edge_weights.shape[0]
    like = jax.ShapeDtypeStruct
    face = like((faces, width), BF)
    lines = 2 * (slots // width)
    packed = like((faces + lines, width), BF)
    *sends, pick, pick_mask, ends = call(
        first_kernel,
        [packed] * 4
        + [like((4, faces, half), BF), like((4, faces, width), BF), like((2, lines, width), BF)],
        (latent_now, tops, bottoms, etop, ebot, live),
        in_specs=[HBM] * 6,
        scratch=[
            pltpu.VMEM((rows, width), BF), pltpu.VMEM(tops.shape, I32),
            pltpu.VMEM(tops.shape, I32), pltpu.VMEM(etop.shape, I32), pltpu.VMEM(etop.shape, I32),
            pltpu.SMEM(live.shape, I32), pltpu.SemaphoreType.DMA((6,)),
        ],
        name="first",
        grant=54 << 20,
    )
    group_like = [
        like((slots, 2 * faces), BF), like((half, slots), BF), like((slots, width), BF)
    ]
    groups = {}
    for step in range(steps):
        starting, last = step == 0, step == steps - 1
        near_x, far_x, near_y, far_y = (sends[place] for place in PLACE)
        got = {
            FAR_Y: swapped(far_y, "gy", 1),
            FAR_X: swapped(far_x, "gx", 1),
            NEAR_Y: swapped(near_y, "gy", 0),
            NEAR_X: swapped(near_x, "gx", 0),
        }
        if starting:
            made = call(
                setup_kernel,
                [like((fanout * rows, half), BF), like((half, fanout * rows), BF),
                 like((fanout * rows, width), BF),
                 like((steps, 2, width, width), BF), like((steps, 2 * width, 2 * width), BF),
                 like((steps, 2 * width, width), BF), like((steps, width, width), BF),
                 like(bias_rows.shape, F32)],
                (nbr, edge_weights, node_weights, bias_rows),
                name="setup",
            )
            inner, (ends_w, hidden, join, out_w, half_biases) = made[:3], made[3:]
            edge_net = (ends_w, hidden, half_biases)
        gathers = () if starting else tuple(groups[link][0] for link in range(4))
        total, *tables = call(
            functools.partial(inner_kernel, step),
            [like((rows, width), F32), like((4, faces, width), BF)]
            + ([] if starting else [like((4, slots, width), F32)]),
            (latent_now, *sends, *edge_net, *inner, *gathers),
            name="inner",
        )
        for links in VISITS:
            final = links == VISITS[-1]
            kernel = functools.partial(cross_kernel, step, links)
            outs = [like((rows, width), F32)]
            operands = [total, *(got[link] for link in links), *edge_net, *tables]
            if final:
                kernel = functools.partial(last_kernel, step, links, last)
                outs = [like((rows, width), BF)] + ([] if last else [face] * 4)
                operands += [latent_now, join, out_w]
            plain = len(outs)
            if starting:
                outs += group_like * len(links)
                operands += [ends, tops, bottoms]
            else:
                operands += [part for link in links for part in groups[link]]
            if final and not last:
                operands += [pick, pick_mask]
            total, *made = call(kernel, outs, operands, name="update" if final else "cross")
            if starting:
                for k, link in enumerate(links):
                    groups[link] = made[plain - 1 + 3 * k :][:3]
            if final:
                latent_now, sends = total, made[: plain - 1]
    return latent_now[None, None]


def solution(mesh):
    return jax.shard_map(
        local,
        mesh=mesh,
        in_specs=(
            P("gx", "gy", None, None),
            P("gx", "gy", None, None),
            P("gx", "gy", None, None),
            P("gx", "gy", None, None),
            P("gx", "gy", None, None),
            P("gx", "gy", None, None),
            P(None, ("gx", "gy")),
            P(),
            P(),
            P(),
        ),
        out_specs=P("gx", "gy", None, None),
        check_vma=False,
    )
```

```python
import functools

import jax
import jax.numpy as jnp
from jax import lax
from jax.experimental import pallas as pl
from jax.experimental.pallas import tpu as pltpu
from jax.sharding import PartitionSpec as P

BF = jnp.bfloat16
F32 = jnp.float32
I32 = jnp.int32
VMEM = pl.BlockSpec(memory_space=pltpu.VMEM)
HBM = pl.BlockSpec(memory_space=pltpu.HBM)

CUT = 128

NEAR_X, FAR_X, NEAR_Y, FAR_Y = range(4)
ORDER = (FAR_Y, NEAR_Y, FAR_X, NEAR_X)
VISITS = ((NEAR_X, FAR_Y), (FAR_X, NEAR_Y))
PLACE = tuple(ORDER.index(link) for link in range(4))


def swapped(block, axis, odd):
    count = lax.axis_size(axis)
    route = []
    for i in range(odd, count, 2):
        j = (i + 1) % count
        route += [(i, j), (j, i)]
    return lax.ppermute(block, axis, route)


def call(kernel, outs, operands, in_specs=None, scratch=(), name=None, grant=40 << 20):
    moved = sum(o.size * o.dtype.itemsize for o in operands)
    return pl.pallas_call(
        kernel,
        out_shape=outs,
        in_specs=in_specs or [VMEM] * len(operands),
        out_specs=[VMEM] * len(outs),
        scratch_shapes=list(scratch),
        compiler_params=pltpu.CompilerParams(vmem_limit_bytes=grant),
        cost_estimate=pl.CostEstimate(flops=1 << 30, bytes_accessed=moved, transcendentals=0),
        name=name,
    )(*operands)


def dot(a, b):
    return jnp.dot(a, b, preferred_element_type=F32)


def half_silu(y):
    return y + y * jnp.tanh(y)


def column_one_hot(row, depth):
    depths = lax.broadcasted_iota(jnp.int16, (depth, row.shape[1]), 0)
    return jnp.where(depths == row.astype(jnp.int16), BF(1), BF(0))


def column_mask(bit, width):
    return jnp.broadcast_to(bit.astype(F32).astype(BF), (width, bit.shape[1])).T


def cut(row, half):
    bit = (row >= half).astype(I32)
    return bit, row - bit * half


def halves(table):
    half = table.shape[0] // 2
    return jnp.concatenate([table[:half], table[half:]], axis=1)


def choose(both, mask):
    width = both.shape[1] // 2
    return jnp.where(mask > 0, both[:, width:], both[:, :width])


def by_half(values, mask):
    upper = values * mask
    return jnp.concatenate([values - upper, upper], axis=1)


def odd_place():
    return lax.axis_index("gx") % 2, lax.axis_index("gy") % 2


def role_of(link):
    return (odd_place()[link // 2] + link % 2) % 2


def in_order(odd, first, second):
    turned = odd == 1
    return jnp.where(turned, second, first), jnp.where(turned, first, second)


def pick_faces(latent, pick_ref, pick_mask_ref, out_refs):
    table = halves(latent)
    rows = [
        choose(dot(pick_ref[face], table), pick_mask_ref[face]).astype(BF) for face in range(4)
    ]
    for d, odd in enumerate(odd_place()):
        near, far = in_order(odd, rows[2 * d], rows[2 * d + 1])
        count = near.shape[0]
        out_refs[PLACE[2 * d]][0:count, :] = near
        out_refs[PLACE[2 * d + 1]][0:count, :] = far


def first_kernel(
    latent_hbm, tops_hbm, bottoms_hbm, etop_hbm, ebot_hbm, live_hbm,
    send_0, send_1, send_2, send_3, pick_ref, pick_mask_ref, ends_ref,
    latent_ref, tops_ref, bottoms_ref, etop_ref, ebot_ref, live_ref, sems,
):
    moves = [
        pltpu.make_async_copy(src, dst, sems.at[i])
        for i, (src, dst) in enumerate((
            (tops_hbm, tops_ref), (bottoms_hbm, bottoms_ref), (latent_hbm, latent_ref),
            (etop_hbm, etop_ref), (ebot_hbm, ebot_ref), (live_hbm, live_ref),
        ))
    ]
    for move in moves:
        move.start()
    half = latent_ref.shape[0] // 2
    width = latent_ref.shape[1]
    moves[0].wait()
    moves[1].wait()
    for face in range(4):
        d, ref = face // 2, (tops_ref, bottoms_ref)[face % 2]
        bit, low = cut(ref[d : d + 1, :], half)
        pick_ref[face] = column_one_hot(low, half).T
        pick_mask_ref[face] = column_mask(bit, width)
    for move in moves[2:]:
        move.wait()
    sends = (send_0, send_1, send_2, send_3)
    pick_faces(latent_ref[...], pick_ref, pick_mask_ref, sends)
    faces = tops_ref.shape[1]
    slots = etop_ref.shape[1]
    lines = slots // width
    for d in range(2):
        live = lax.broadcasted_iota(I32, (1, slots), 1) < live_ref[0, d]
        etop = etop_ref[d : d + 1, :].astype(F32)
        ebot = jnp.where(live, ebot_ref[d : d + 1, :], -1).astype(F32)
        rows = [v[:, i * width : (i + 1) * width] for v in (etop, ebot) for i in range(lines)]
        ends = jnp.concatenate(rows, axis=0).astype(BF)
        ends_ref[d] = ends
        sends[PLACE[2 * d]][faces:, :] = ends
        sends[PLACE[2 * d + 1]][faces:, :] = ends


def unpacked(ends):
    ends = ends.astype(F32)
    lines = ends.shape[0] // 2

    def row(start):
        parts = [ends[start + i : start + i + 1, :] for i in range(lines)]
        return jnp.concatenate(parts, axis=1).astype(I32)

    return row(0), row(lines)


def link_group(link, got_ref, ends_ref, tops_ref, bottoms_ref, half):
    d = link // 2
    owned = role_of(link) == 0
    faces = tops_ref.shape[1]
    width = got_ref.shape[1]
    etop, ebot = unpacked(jnp.where(owned, ends_ref[d], got_ref[faces:, :]))
    face = jnp.where(owned, tops_ref[d : d + 1, :], bottoms_ref[d : d + 1, :])
    here = column_one_hot(jnp.where(owned, etop, ebot), faces)
    there = column_one_hot(jnp.where(owned, ebot, etop), faces)
    bit, low = cut(face, half)
    lines = jnp.concatenate([low, bit, jnp.zeros((6, faces), I32)], axis=0)
    rows = dot(lines.astype(F32).astype(BF), here).astype(I32)
    low, bit = rows[0:1, :], rows[1:2, :]
    ones = column_one_hot(jnp.where(ebot >= 0, low, -1), half)
    gather = jnp.concatenate([here, there], axis=0).T
    return gather, jnp.where(owned, ones, -ones), column_mask(bit, width)


def link_first(step, link, got_ref, gather, ends_w_ref, biases_ref, table_ref, ahead_ref):
    role = role_of(link)
    faces = table_ref.shape[1]
    far = dot(got_ref[0:faces, :], ends_w_ref[step, 1 - role]).astype(BF)
    if step > 0:
        y = dot(gather[:, faces:], far) + ahead_ref[link]
    else:
        table = jnp.concatenate([table_ref[link], far], axis=0)
        y = dot(gather, table) + biases_ref[0, step : step + 1, :]
    return half_silu(y).astype(BF)


def second_layer(first, weight, bias):
    parts = [
        half_silu(dot(first[a : a + CUT], weight) + bias).astype(BF)
        for a in range(0, first.shape[0], CUT)
    ]
    return jnp.concatenate(parts, axis=0)


def placed(places, values):
    parts = []
    for a in range(0, places[0].shape[0], CUT):
        part = None
        for place, value in zip(places, values):
            product = dot(place[a : a + CUT], value)
            part = product if part is None else part + product
        parts.append(part)
    return jnp.concatenate(parts, axis=0)


def link_sums(step, links, gots, groups, ends_w_ref, hidden_ref, biases_ref, table_ref, ahead_ref):
    width = ends_w_ref.shape[2]
    wide = width * len(links)
    first = [
        link_first(step, link, got, group[0], ends_w_ref, biases_ref, table_ref, ahead_ref)
        for link, got, group in zip(links, gots, groups)
    ]
    bias = biases_ref[1, step : step + 1, :]
    second = second_layer(
        jnp.concatenate(first, axis=1),
        hidden_ref[step, 0:wide, 0:wide],
        jnp.concatenate([bias] * len(links), axis=1),
    )
    values = [
        by_half(second[:, i * width : (i + 1) * width], group[2]) for i, group in enumerate(groups)
    ]
    return placed([group[1] for group in groups], values)


def prepared(step, links, got_refs, refs, half):
    count = 3 * len(links)
    if step > 0:
        kept, rest = refs[:count], refs[count:]
    else:
        kept, rest = refs[-count:], refs[3:-count]
        for i, (link, got_ref) in enumerate(zip(links, got_refs)):
            for ref, value in zip(kept[3 * i :], link_group(link, got_ref, *refs[:3], half)):
                ref[...] = value
    return [tuple(ref[...] for ref in kept[i : i + 3]) for i in range(0, count, 3)], rest


def setup_kernel(
    nbr_ref, weights_ref, nodes_ref, raw_biases_ref,
    pick_ref, spread_ref, mask_ref, ends_w_ref, hidden_ref, join_ref, out_w_ref, biases_ref,
):
    half = spread_ref.shape[0]
    width = mask_ref.shape[1]
    rows = nbr_ref.shape[1]
    for k in range(nbr_ref.shape[0]):
        here = slice(k * rows, (k + 1) * rows)
        bit, low = cut(nbr_ref[k : k + 1, :], half)
        ones = column_one_hot(low, half)
        pick_ref[here, :] = ones.T
        spread_ref[:, here] = -ones
        mask_ref[here, :] = column_mask(bit, width)
    biases_ref[...] = raw_biases_ref[...] * 0.5
    zero = jnp.zeros((width, width), BF)
    for step in range(weights_ref.shape[0]):
        ends_w_ref[step, 0] = weights_ref[step, 0] * BF(0.5)
        ends_w_ref[step, 1] = weights_ref[step, 1] * BF(0.5)
        hidden = weights_ref[step, 2] * BF(0.5)
        hidden_ref[step] = jnp.concatenate(
            [jnp.concatenate([hidden, zero], axis=1), jnp.concatenate([zero, hidden], axis=1)],
            axis=0,
        )
        fold = dot(weights_ref[step, 3], nodes_ref[step, 1]).astype(BF)
        join_ref[step] = jnp.concatenate([nodes_ref[step, 0], fold], axis=0) * BF(0.5)
        out_w_ref[step] = nodes_ref[step, 2]


def inner_kernel(
    step, latent_ref, send_0, send_1, send_2, send_3, ends_w_ref, hidden_ref, biases_ref,
    pick_ref, spread_ref, mask_ref, *refs,
):
    rows, width = latent_ref.shape
    half = rows // 2
    sends = (send_0, send_1, send_2, send_3)
    if step > 0:
        gather_refs, (total_ref, table_ref, ahead_ref) = refs[:4], refs[4:]
    else:
        total_ref, table_ref = refs
    faces = table_ref.shape[1]
    for link in range(4):
        face = sends[PLACE[link]][0:faces, :]
        table_ref[link] = dot(face, ends_w_ref[step, role_of(link)]).astype(BF)
    latent = latent_ref[...]
    source = dot(latent, ends_w_ref[step, 0]) + biases_ref[0, step : step + 1, :]
    table = halves(dot(latent, ends_w_ref[step, 1]).astype(BF))
    c1 = biases_ref[1, step : step + 1, :]
    c1 = jnp.concatenate([c1, c1], axis=1)
    fanout = pick_ref.shape[0] // rows
    total = None
    ended = None
    for pair in range(0, fanout, 2):
        here = [slice(k * rows, (k + 1) * rows) for k in (pair, pair + 1)]
        first = [
            half_silu(choose(dot(pick_ref[k, :], table), mask_ref[k, :]) + source).astype(BF)
            for k in here
        ]
        first = jnp.concatenate(first, axis=1)
        second = [
            half_silu(dot(first[a : a + CUT], hidden_ref[step]) + c1) for a in range(0, rows, CUT)
        ]
        started = jnp.concatenate([q[:, :width] + q[:, width:] for q in second], axis=0)
        total = started if total is None else total + started
        second = jnp.concatenate([q.astype(BF) for q in second], axis=0)
        values = [
            by_half(second[:, i * width : (i + 1) * width], mask_ref[k, :])
            for i, k in enumerate(here)
        ]
        part = jnp.concatenate(
            [dot(spread_ref[a : a + CUT, here[0]], values[0])
             + dot(spread_ref[a : a + CUT, here[1]], values[1]) for a in range(0, half, CUT)],
            axis=0,
        )
        ended = part if ended is None else ended + part
    total_ref[0:half, :] = total[0:half] + ended[:, :width]
    total_ref[half:, :] = total[half:] + ended[:, width:]
    if step > 0:
        c0 = biases_ref[0, step : step + 1, :]
        for link, ref in enumerate(gather_refs):
            ahead_ref[link] = dot(ref[:, 0:faces], table_ref[link]) + c0


def cross_kernel(step, links, total_ref, *refs):
    rows, width = total_ref.shape
    half = rows // 2
    gots, refs = refs[: len(links)], refs[len(links) :]
    nets, refs = refs[: 4 + (step > 0)], refs[4 + (step > 0) :]
    groups, (out_ref,) = prepared(step, links, gots, refs, half)
    ahead_ref = nets[4] if step > 0 else None
    both = link_sums(step, links, gots, groups, *nets[:4], ahead_ref)
    out_ref[0:half, :] = total_ref[0:half, :] + both[:, :width]
    out_ref[half:, :] = total_ref[half:, :] + both[:, width:]


def last_kernel(step, links, last, total_ref, *refs):
    rows, width = total_ref.shape
    half = rows // 2
    gots, refs = refs[: len(links)], refs[len(links) :]
    nets, refs = refs[: 4 + (step > 0)], refs[4 + (step > 0) :]
    (latent_ref, join_ref, out_w_ref), refs = refs[:3], refs[3:]
    groups, rest = prepared(step, links, gots, refs, half)
    ahead_ref = nets[4] if step > 0 else None
    biases_ref = nets[2]
    both = link_sums(step, links, gots, groups, *nets[:4], ahead_ref)
    arrived = total_ref[...] + jnp.concatenate([both[:, :width], both[:, width:]], axis=0)
    latent = latent_ref[...]
    joined = jnp.concatenate([latent, arrived.astype(BF)], axis=1)
    update = half_silu(dot(joined, join_ref[step]) + biases_ref[2, step : step + 1, :]).astype(BF)
    latent = (latent.astype(F32) + dot(update, out_w_ref[step])).astype(BF)
    if last:
        rest[0][...] = latent
    else:
        pick_ref, pick_mask_ref, out_ref = rest[:3]
        out_ref[...] = latent
        pick_faces(latent, pick_ref, pick_mask_ref, rest[3:7])


def local(
    latent,
    neighbours,
    top_rows,
    bottom_rows,
    edge_top,
    edge_bottom,
    live_count,
    edge_weights,
    node_weights,
    biases,
):
    latent_now = latent[0, 0]
    rows, width = latent_now.shape
    half = rows // 2
    nbr = neighbours[0, 0]
    tops = top_rows[0, 0]
    bottoms = bottom_rows[0, 0]
    etop = edge_top[0, 0]
    ebot = edge_bottom[0, 0]
    live = live_count.T
    bias_rows = jnp.swapaxes(biases, 0, 1)
    fanout = nbr.shape[0]
    faces = tops.shape[1]
    slots = etop.shape[1]
    steps = edge_weights.shape[0]
    like = jax.ShapeDtypeStruct
    face = like((faces, width), BF)
    lines = 2 * (slots // width)
    packed = like((faces + lines, width), BF)
    *sends, pick, pick_mask, ends = call(
        first_kernel,
        [packed] * 4
        + [like((4, faces, half), BF), like((4, faces, width), BF), like((2, lines, width), BF)],
        (latent_now, tops, bottoms, etop, ebot, live),
        in_specs=[HBM] * 6,
        scratch=[
            pltpu.VMEM((rows, width), BF), pltpu.VMEM(tops.shape, I32),
            pltpu.VMEM(tops.shape, I32), pltpu.VMEM(etop.shape, I32), pltpu.VMEM(etop.shape, I32),
            pltpu.SMEM(live.shape, I32), pltpu.SemaphoreType.DMA((6,)),
        ],
        name="first",
        grant=54 << 20,
    )
    group_like = [
        like((slots, 2 * faces), BF), like((half, slots), BF), like((slots, width), BF)
    ]
    groups = {}
    for step in range(steps):
        starting, last = step == 0, step == steps - 1
        near_x, far_x, near_y, far_y = (sends[place] for place in PLACE)
        got = {
            FAR_Y: swapped(far_y, "gy", 1),
            FAR_X: swapped(far_x, "gx", 1),
            NEAR_Y: swapped(near_y, "gy", 0),
            NEAR_X: swapped(near_x, "gx", 0),
        }
        if starting:
            made = call(
                setup_kernel,
                [like((fanout * rows, half), BF), like((half, fanout * rows), BF),
                 like((fanout * rows, width), BF),
                 like((steps, 2, width, width), BF), like((steps, 2 * width, 2 * width), BF),
                 like((steps, 2 * width, width), BF), like((steps, width, width), BF),
                 like(bias_rows.shape, F32)],
                (nbr, edge_weights, node_weights, bias_rows),
                name="setup",
            )
            inner, (ends_w, hidden, join, out_w, half_biases) = made[:3], made[3:]
            edge_net = (ends_w, hidden, half_biases)
        gathers = () if starting else tuple(groups[link][0] for link in range(4))
        total, *tables = call(
            functools.partial(inner_kernel, step),
            [like((rows, width), F32), like((4, faces, width), BF)]
            + ([] if starting else [like((4, slots, width), F32)]),
            (latent_now, *sends, *edge_net, *inner, *gathers),
            name="inner",
        )
        for links in VISITS:
            final = links == VISITS[-1]
            kernel = functools.partial(cross_kernel, step, links)
            outs = [like((rows, width), F32)]
            operands = [total, *(got[link] for link in links), *edge_net, *tables]
            if final:
                kernel = functools.partial(last_kernel, step, links, last)
                outs = [like((rows, width), BF)] + ([] if last else [face] * 4)
                operands += [latent_now, join, out_w]
            plain = len(outs)
            if starting:
                outs += group_like * len(links)
                operands += [ends, tops, bottoms]
            else:
                operands += [part for link in links for part in groups[link]]
            if final and not last:
                operands += [pick, pick_mask]
            total, *made = call(kernel, outs, operands, name="update" if final else "cross")
            if starting:
                for k, link in enumerate(links):
                    groups[link] = made[plain - 1 + 3 * k :][:3]
            if final:
                latent_now, sends = total, made[: plain - 1]
    return latent_now[None, None]


def solution(mesh):
    return jax.shard_map(
        local,
        mesh=mesh,
        in_specs=(
            P("gx", "gy", None, None),
            P("gx", "gy", None, None),
            P("gx", "gy", None, None),
            P("gx", "gy", None, None),
            P("gx", "gy", None, None),
            P("gx", "gy", None, None),
            P(None, ("gx", "gy")),
            P(),
            P(),
            P(),
        ),
        out_specs=P("gx", "gy", None, None),
        check_vma=False,
    )
```

```python
import functools

import jax
import jax.numpy as jnp
from jax import lax
from jax.experimental import pallas as pl
from jax.experimental.pallas import tpu as pltpu
from jax.sharding import PartitionSpec as P

BF = jnp.bfloat16
F32 = jnp.float32
I32 = jnp.int32
VMEM = pl.BlockSpec(memory_space=pltpu.VMEM)
HBM = pl.BlockSpec(memory_space=pltpu.HBM)

CUT = 128

NEAR_X, FAR_X, NEAR_Y, FAR_Y = range(4)
ORDER = (NEAR_Y, FAR_Y, FAR_X, NEAR_X)
VISITS = ((NEAR_X, NEAR_Y), (FAR_X, FAR_Y))
PLACE = tuple(ORDER.index(link) for link in range(4))


def swapped(block, axis, odd):
    count = lax.axis_size(axis)
    route = []
    for i in range(odd, count, 2):
        j = (i + 1) % count
        route += [(i, j), (j, i)]
    return lax.ppermute(block, axis, route)


def call(
    kernel, outs, operands, in_specs=None, out_specs=None, scratch=(), name=None, grant=40 << 20
):
    moved = sum(o.size * o.dtype.itemsize for o in operands)
    return pl.pallas_call(
        kernel,
        out_shape=outs,
        in_specs=in_specs or [VMEM] * len(operands),
        out_specs=out_specs or [VMEM] * len(outs),
        scratch_shapes=list(scratch),
        compiler_params=pltpu.CompilerParams(vmem_limit_bytes=grant),
        cost_estimate=pl.CostEstimate(flops=1 << 30, bytes_accessed=moved, transcendentals=0),
        name=name,
    )(*operands)


def dot(a, b):
    return jnp.dot(a, b, preferred_element_type=F32)


def half_silu(y):
    return y + y * jnp.tanh(y)


def column_one_hot(row, depth):
    depths = lax.broadcasted_iota(jnp.int16, (depth, row.shape[1]), 0)
    return jnp.where(depths == row.astype(jnp.int16), BF(1), BF(0))


def column_mask(bit, width):
    return jnp.broadcast_to(bit.astype(F32).astype(BF), (width, bit.shape[1])).T


def cut(row, half):
    bit = (row >= half).astype(I32)
    return bit, row - bit * half


def halves(table):
    half = table.shape[0] // 2
    return jnp.concatenate([table[:half], table[half:]], axis=1)


def choose(both, mask):
    width = both.shape[1] // 2
    return jnp.where(mask > 0, both[:, width:], both[:, :width])


def by_half(values, mask):
    upper = values * mask
    return jnp.concatenate([values - upper, upper], axis=1)


def odd_place():
    return lax.axis_index("gx") % 2, lax.axis_index("gy") % 2


def role_of(link):
    return (odd_place()[link // 2] + link % 2) % 2


def in_order(odd, first, second):
    turned = odd == 1
    return jnp.where(turned, second, first), jnp.where(turned, first, second)


def pick_faces(latent, pick_ref, pick_mask_ref, out_refs):
    table = halves(latent)
    rows = [
        choose(dot(pick_ref[face], table), pick_mask_ref[face]).astype(BF) for face in range(4)
    ]
    for d, odd in enumerate(odd_place()):
        near, far = in_order(odd, rows[2 * d], rows[2 * d + 1])
        count = near.shape[0]
        out_refs[PLACE[2 * d]][0:count, :] = near
        out_refs[PLACE[2 * d + 1]][0:count, :] = far


def first_kernel(
    latent_hbm, tops_hbm, bottoms_hbm, etop_hbm, ebot_hbm, live_hbm,
    out_0, out_1, out_2, out_3, out_pick, out_pick_mask, out_ends,
    send_0, send_1, send_2, send_3, pick_ref, pick_mask_ref, ends_ref,
    latent_ref, tops_ref, bottoms_ref, etop_ref, ebot_ref, live_ref, sems,
):
    moves = [
        pltpu.make_async_copy(src, dst, sems.at[i])
        for i, (src, dst) in enumerate((
            (tops_hbm, tops_ref), (bottoms_hbm, bottoms_ref), (latent_hbm, latent_ref),
            (etop_hbm, etop_ref), (ebot_hbm, ebot_ref), (live_hbm, live_ref),
            (pick_ref, out_pick), (pick_mask_ref, out_pick_mask),
            (send_0, out_0), (send_1, out_1), (send_2, out_2), (send_3, out_3),
            (ends_ref, out_ends),
        ))
    ]
    for move in moves[:6]:
        move.start()
    half = latent_ref.shape[0] // 2
    width = latent_ref.shape[1]
    sends = (send_0, send_1, send_2, send_3)
    moves[0].wait()
    moves[1].wait()
    for face in range(4):
        d, ref = face // 2, (tops_ref, bottoms_ref)[face % 2]
        bit, low = cut(ref[d : d + 1, :], half)
        pick_ref[face] = column_one_hot(low, half).T
        pick_mask_ref[face] = column_mask(bit, width)
    for move in moves[2:6]:
        move.wait()
    for move in moves[6:8]:
        move.start()
    pick_faces(latent_ref[...], pick_ref, pick_mask_ref, sends)
    faces = tops_ref.shape[1]
    slots = etop_ref.shape[1]
    lines = slots // width
    for d in range(2):
        live = lax.broadcasted_iota(I32, (1, slots), 1) < live_ref[0, d]
        etop = etop_ref[d : d + 1, :].astype(F32)
        ebot = jnp.where(live, ebot_ref[d : d + 1, :], -1).astype(F32)
        rows = [v[:, i * width : (i + 1) * width] for v in (etop, ebot) for i in range(lines)]
        ends = jnp.concatenate(rows, axis=0).astype(BF)
        ends_ref[d] = ends
        sends[PLACE[2 * d]][faces:, :] = ends
        sends[PLACE[2 * d + 1]][faces:, :] = ends
    for move in moves[8:]:
        move.start()
    for move in moves[6:]:
        move.wait()


def unpacked(ends):
    ends = ends.astype(F32)
    lines = ends.shape[0] // 2

    def row(start):
        parts = [ends[start + i : start + i + 1, :] for i in range(lines)]
        return jnp.concatenate(parts, axis=1).astype(I32)

    return row(0), row(lines)


def link_group(link, got_ref, ends_ref, tops_ref, bottoms_ref, half):
    d = link // 2
    owned = role_of(link) == 0
    faces = tops_ref.shape[1]
    width = got_ref.shape[1]
    etop, ebot = unpacked(jnp.where(owned, ends_ref[d], got_ref[faces:, :]))
    face = jnp.where(owned, tops_ref[d : d + 1, :], bottoms_ref[d : d + 1, :])
    here = column_one_hot(jnp.where(owned, etop, ebot), faces)
    there = column_one_hot(jnp.where(owned, ebot, etop), faces)
    bit, low = cut(face, half)
    lines = jnp.concatenate([low, bit, jnp.zeros((6, faces), I32)], axis=0)
    rows = dot(lines.astype(F32).astype(BF), here).astype(I32)
    low, bit = rows[0:1, :], rows[1:2, :]
    ones = column_one_hot(jnp.where(ebot >= 0, low, -1), half)
    gather = jnp.concatenate([here, there], axis=0).T
    return gather, jnp.where(owned, ones, -ones), column_mask(bit, width)


def link_first(step, link, got_ref, gather, ends_w_ref, biases_ref, table_ref, ahead_ref):
    role = role_of(link)
    faces = table_ref.shape[1]
    far = dot(got_ref[0:faces, :], ends_w_ref[step, 1 - role]).astype(BF)
    if step > 0:
        y = dot(gather[:, faces:], far) + ahead_ref[link]
    else:
        table = jnp.concatenate([table_ref[link], far], axis=0)
        y = dot(gather, table) + biases_ref[0, step : step + 1, :]
    return half_silu(y).astype(BF)


def second_layer(first, weight, bias):
    parts = [
        half_silu(dot(first[a : a + CUT], weight) + bias).astype(BF)
        for a in range(0, first.shape[0], CUT)
    ]
    return jnp.concatenate(parts, axis=0)


def placed(places, values):
    parts = []
    for a in range(0, places[0].shape[0], CUT):
        part = None
        for place, value in zip(places, values):
            product = dot(place[a : a + CUT], value)
            part = product if part is None else part + product
        parts.append(part)
    return jnp.concatenate(parts, axis=0)


def link_sums(step, links, gots, groups, ends_w_ref, hidden_ref, biases_ref, table_ref, ahead_ref):
    width = ends_w_ref.shape[2]
    wide = width * len(links)
    first = [
        link_first(step, link, got, group[0], ends_w_ref, biases_ref, table_ref, ahead_ref)
        for link, got, group in zip(links, gots, groups)
    ]
    bias = biases_ref[1, step : step + 1, :]
    second = second_layer(
        jnp.concatenate(first, axis=1),
        hidden_ref[step, 0:wide, 0:wide],
        jnp.concatenate([bias] * len(links), axis=1),
    )
    values = [
        by_half(second[:, i * width : (i + 1) * width], group[2]) for i, group in enumerate(groups)
    ]
    return placed([group[1] for group in groups], values)


def prepared(step, links, got_refs, refs, half):
    count = 3 * len(links)
    if step > 0:
        kept, rest = refs[:count], refs[count:]
    else:
        kept, rest = refs[-count:], refs[3:-count]
        for i, (link, got_ref) in enumerate(zip(links, got_refs)):
            for ref, value in zip(kept[3 * i :], link_group(link, got_ref, *refs[:3], half)):
                ref[...] = value
    return [tuple(ref[...] for ref in kept[i : i + 3]) for i in range(0, count, 3)], rest


def setup_kernel(
    nbr_ref, weights_ref, nodes_ref, raw_biases_ref,
    pick_ref, spread_ref, mask_ref, ends_w_ref, hidden_ref, join_ref, out_w_ref, biases_ref,
):
    half = spread_ref.shape[0]
    width = mask_ref.shape[1]
    rows = nbr_ref.shape[1]
    for k in range(nbr_ref.shape[0]):
        here = slice(k * rows, (k + 1) * rows)
        bit, low = cut(nbr_ref[k : k + 1, :], half)
        ones = column_one_hot(low, half)
        pick_ref[here, :] = ones.T
        spread_ref[:, here] = -ones
        mask_ref[here, :] = column_mask(bit, width)
    biases_ref[...] = raw_biases_ref[...] * 0.5
    zero = jnp.zeros((width, width), BF)
    for step in range(weights_ref.shape[0]):
        ends_w_ref[step, 0] = weights_ref[step, 0] * BF(0.5)
        ends_w_ref[step, 1] = weights_ref[step, 1] * BF(0.5)
        hidden = weights_ref[step, 2] * BF(0.5)
        hidden_ref[step] = jnp.concatenate(
            [jnp.concatenate([hidden, zero], axis=1), jnp.concatenate([zero, hidden], axis=1)],
            axis=0,
        )
        fold = dot(weights_ref[step, 3], nodes_ref[step, 1]).astype(BF)
        join_ref[step] = jnp.concatenate([nodes_ref[step, 0], fold], axis=0) * BF(0.5)
        out_w_ref[step] = nodes_ref[step, 2]


def inner_kernel(
    step, latent_ref, send_0, send_1, send_2, send_3, ends_w_ref, hidden_ref, biases_ref,
    pick_ref, spread_ref, mask_ref, *refs,
):
    rows, width = latent_ref.shape
    half = rows // 2
    sends = (send_0, send_1, send_2, send_3)
    if step > 0:
        gather_refs, (total_ref, table_ref, ahead_ref) = refs[:4], refs[4:]
    else:
        total_ref, table_ref = refs
    faces = table_ref.shape[1]
    for link in range(4):
        face = sends[PLACE[link]][0:faces, :]
        table_ref[link] = dot(face, ends_w_ref[step, role_of(link)]).astype(BF)
    latent = latent_ref[...]
    source = dot(latent, ends_w_ref[step, 0]) + biases_ref[0, step : step + 1, :]
    table = halves(dot(latent, ends_w_ref[step, 1]).astype(BF))
    c1 = biases_ref[1, step : step + 1, :]
    c1 = jnp.concatenate([c1, c1], axis=1)
    fanout = pick_ref.shape[0] // rows
    total = None
    ended = None
    for pair in range(0, fanout, 2):
        here = [slice(k * rows, (k + 1) * rows) for k in (pair, pair + 1)]
        first = [
            half_silu(choose(dot(pick_ref[k, :], table), mask_ref[k, :]) + source).astype(BF)
            for k in here
        ]
        first = jnp.concatenate(first, axis=1)
        second = [
            half_silu(dot(first[a : a + CUT], hidden_ref[step]) + c1) for a in range(0, rows, CUT)
        ]
        started = jnp.concatenate([q[:, :width] + q[:, width:] for q in second], axis=0)
        total = started if total is None else total + started
        second = jnp.concatenate([q.astype(BF) for q in second], axis=0)
        values = [
            by_half(second[:, i * width : (i + 1) * width], mask_ref[k, :])
            for i, k in enumerate(here)
        ]
        part = jnp.concatenate(
            [dot(spread_ref[a : a + CUT, here[0]], values[0])
             + dot(spread_ref[a : a + CUT, here[1]], values[1]) for a in range(0, half, CUT)],
            axis=0,
        )
        ended = part if ended is None else ended + part
    total_ref[0:half, :] = total[0:half] + ended[:, :width]
    total_ref[half:, :] = total[half:] + ended[:, width:]
    if step > 0:
        c0 = biases_ref[0, step : step + 1, :]
        for link, ref in enumerate(gather_refs):
            ahead_ref[link] = dot(ref[:, 0:faces], table_ref[link]) + c0


def cross_kernel(step, links, total_ref, *refs):
    rows, width = total_ref.shape
    half = rows // 2
    gots, refs = refs[: len(links)], refs[len(links) :]
    nets, refs = refs[: 4 + (step > 0)], refs[4 + (step > 0) :]
    groups, (out_ref,) = prepared(step, links, gots, refs, half)
    ahead_ref = nets[4] if step > 0 else None
    both = link_sums(step, links, gots, groups, *nets[:4], ahead_ref)
    out_ref[0:half, :] = total_ref[0:half, :] + both[:, :width]
    out_ref[half:, :] = total_ref[half:, :] + both[:, width:]


def last_kernel(step, links, last, total_ref, *refs):
    rows, width = total_ref.shape
    half = rows // 2
    gots, refs = refs[: len(links)], refs[len(links) :]
    nets, refs = refs[: 4 + (step > 0)], refs[4 + (step > 0) :]
    (latent_ref, join_ref, out_w_ref), refs = refs[:3], refs[3:]
    groups, rest = prepared(step, links, gots, refs, half)
    ahead_ref = nets[4] if step > 0 else None
    biases_ref = nets[2]
    both = link_sums(step, links, gots, groups, *nets[:4], ahead_ref)
    arrived = total_ref[...] + jnp.concatenate([both[:, :width], both[:, width:]], axis=0)
    latent = latent_ref[...]
    joined = jnp.concatenate([latent, arrived.astype(BF)], axis=1)
    update = half_silu(dot(joined, join_ref[step]) + biases_ref[2, step : step + 1, :]).astype(BF)
    latent = (latent.astype(F32) + dot(update, out_w_ref[step])).astype(BF)
    if last:
        rest[0][...] = latent
    else:
        pick_ref, pick_mask_ref, out_ref = rest[:3]
        out_ref[...] = latent
        pick_faces(latent, pick_ref, pick_mask_ref, rest[3:7])


def local(
    latent,
    neighbours,
    top_rows,
    bottom_rows,
    edge_top,
    edge_bottom,
    live_count,
    edge_weights,
    node_weights,
    biases,
):
    latent_now = latent[0, 0]
    rows, width = latent_now.shape
    half = rows // 2
    nbr = neighbours[0, 0]
    tops = top_rows[0, 0]
    bottoms = bottom_rows[0, 0]
    etop = edge_top[0, 0]
    ebot = edge_bottom[0, 0]
    live = live_count.T
    bias_rows = jnp.swapaxes(biases, 0, 1)
    fanout = nbr.shape[0]
    faces = tops.shape[1]
    slots = etop.shape[1]
    steps = edge_weights.shape[0]
    like = jax.ShapeDtypeStruct
    face = like((faces, width), BF)
    lines = 2 * (slots // width)
    packed = like((faces + lines, width), BF)
    *sends, pick, pick_mask, ends = call(
        first_kernel,
        [packed] * 4
        + [like((4, faces, half), BF), like((4, faces, width), BF), like((2, lines, width), BF)],
        (latent_now, tops, bottoms, etop, ebot, live),
        in_specs=[HBM] * 6,
        out_specs=[HBM] * 7,
        scratch=[pltpu.VMEM(packed.shape, BF)] * 4 + [
            pltpu.VMEM((4, faces, half), BF), pltpu.VMEM((4, faces, width), BF),
            pltpu.VMEM((2, lines, width), BF),
            pltpu.VMEM((rows, width), BF), pltpu.VMEM(tops.shape, I32),
            pltpu.VMEM(tops.shape, I32), pltpu.VMEM(etop.shape, I32), pltpu.VMEM(etop.shape, I32),
            pltpu.SMEM(live.shape, I32), pltpu.SemaphoreType.DMA((13,)),
        ],
        name="first",
        grant=54 << 20,
    )
    group_like = [
        like((slots, 2 * faces), BF), like((half, slots), BF), like((slots, width), BF)
    ]
    groups = {}
    for step in range(steps):
        starting, last = step == 0, step == steps - 1
        near_x, far_x, near_y, far_y = (sends[place] for place in PLACE)
        got = {
            FAR_Y: swapped(far_y, "gy", 1),
            FAR_X: swapped(far_x, "gx", 1),
            NEAR_Y: swapped(near_y, "gy", 0),
            NEAR_X: swapped(near_x, "gx", 0),
        }
        if starting:
            made = call(
                setup_kernel,
                [like((fanout * rows, half), BF), like((half, fanout * rows), BF),
                 like((fanout * rows, width), BF),
                 like((steps, 2, width, width), BF), like((steps, 2 * width, 2 * width), BF),
                 like((steps, 2 * width, width), BF), like((steps, width, width), BF),
                 like(bias_rows.shape, F32)],
                (nbr, edge_weights, node_weights, bias_rows),
                name="setup",
            )
            inner, (ends_w, hidden, join, out_w, half_biases) = made[:3], made[3:]
            edge_net = (ends_w, hidden, half_biases)
        gathers = () if starting else tuple(groups[link][0] for link in range(4))
        total, *tables = call(
            functools.partial(inner_kernel, step),
            [like((rows, width), F32), like((4, faces, width), BF)]
            + ([] if starting else [like((4, slots, width), F32)]),
            (latent_now, *sends, *edge_net, *inner, *gathers),
            name="inner",
        )
        for links in VISITS:
            final = links == VISITS[-1]
            kernel = functools.partial(cross_kernel, step, links)
            outs = [like((rows, width), F32)]
            operands = [total, *(got[link] for link in links), *edge_net, *tables]
            if final:
                kernel = functools.partial(last_kernel, step, links, last)
                outs = [like((rows, width), BF)] + ([] if last else [face] * 4)
                operands += [latent_now, join, out_w]
            plain = len(outs)
            if starting:
                outs += group_like * len(links)
                operands += [ends, tops, bottoms]
            else:
                operands += [part for link in links for part in groups[link]]
            if final and not last:
                operands += [pick, pick_mask]
            total, *made = call(kernel, outs, operands, name="update" if final else "cross")
            if starting:
                for k, link in enumerate(links):
                    groups[link] = made[plain - 1 + 3 * k :][:3]
            if final:
                latent_now, sends = total, made[: plain - 1]
    return latent_now[None, None]


def solution(mesh):
    return jax.shard_map(
        local,
        mesh=mesh,
        in_specs=(
            P("gx", "gy", None, None),
            P("gx", "gy", None, None),
            P("gx", "gy", None, None),
            P("gx", "gy", None, None),
            P("gx", "gy", None, None),
            P("gx", "gy", None, None),
            P(None, ("gx", "gy")),
            P(),
            P(),
            P(),
        ),
        out_specs=P("gx", "gy", None, None),
        check_vma=False,
    )
```

```python
import functools

import jax
import jax.numpy as jnp
from jax import lax
from jax.experimental import pallas as pl
from jax.experimental.pallas import tpu as pltpu
from jax.sharding import PartitionSpec as P

BF = jnp.bfloat16
F32 = jnp.float32
I32 = jnp.int32
VMEM = pl.BlockSpec(memory_space=pltpu.VMEM)
HBM = pl.BlockSpec(memory_space=pltpu.HBM)

CUT = 128

NEAR_X, FAR_X, NEAR_Y, FAR_Y = range(4)
ORDER = (NEAR_Y, FAR_Y, FAR_X, NEAR_X)
VISITS = ((NEAR_X, NEAR_Y), (FAR_X, FAR_Y))
PLACE = tuple(ORDER.index(link) for link in range(4))


def swapped(block, axis, odd):
    count = lax.axis_size(axis)
    route = []
    for i in range(odd, count, 2):
        j = (i + 1) % count
        route += [(i, j), (j, i)]
    return lax.ppermute(block, axis, route)


def call(
    kernel, outs, operands, in_specs=None, out_specs=None, scratch=(), name=None, grant=40 << 20
):
    moved = sum(o.size * o.dtype.itemsize for o in operands)
    return pl.pallas_call(
        kernel,
        out_shape=outs,
        in_specs=in_specs or [VMEM] * len(operands),
        out_specs=out_specs or [VMEM] * len(outs),
        scratch_shapes=list(scratch),
        compiler_params=pltpu.CompilerParams(vmem_limit_bytes=grant),
        cost_estimate=pl.CostEstimate(flops=1 << 30, bytes_accessed=moved, transcendentals=0),
        name=name,
    )(*operands)


def dot(a, b):
    return jnp.dot(a, b, preferred_element_type=F32)


def half_silu(y):
    return y + y * jnp.tanh(y)


def column_one_hot(row, depth):
    depths = lax.broadcasted_iota(jnp.int16, (depth, row.shape[1]), 0)
    return jnp.where(depths == row.astype(jnp.int16), BF(1), BF(0))


def column_mask(bit, width):
    return jnp.broadcast_to(bit.astype(F32).astype(BF), (width, bit.shape[1])).T


def cut(row, half):
    bit = (row >= half).astype(I32)
    return bit, row - bit * half


def halves(table):
    half = table.shape[0] // 2
    return jnp.concatenate([table[:half], table[half:]], axis=1)


def choose(both, mask):
    width = both.shape[1] // 2
    return jnp.where(mask > 0, both[:, width:], both[:, :width])


def by_half(values, mask):
    upper = values * mask
    return jnp.concatenate([values - upper, upper], axis=1)


def odd_place():
    return lax.axis_index("gx") % 2, lax.axis_index("gy") % 2


def role_of(link):
    return (odd_place()[link // 2] + link % 2) % 2


def in_order(odd, first, second):
    turned = odd == 1
    return jnp.where(turned, second, first), jnp.where(turned, first, second)


def pick_faces(latent, pick_ref, pick_mask_ref, out_refs):
    table = halves(latent)
    rows = [
        choose(dot(pick_ref[face], table), pick_mask_ref[face]).astype(BF) for face in range(4)
    ]
    for d, odd in enumerate(odd_place()):
        near, far = in_order(odd, rows[2 * d], rows[2 * d + 1])
        count = near.shape[0]
        out_refs[PLACE[2 * d]][0:count, :] = near
        out_refs[PLACE[2 * d + 1]][0:count, :] = far


def first_kernel(
    latent_hbm, tops_hbm, bottoms_hbm, etop_hbm, ebot_hbm, live_hbm,
    out_0, out_1, out_2, out_3, out_pick, out_pick_mask, out_ends,
    send_0, send_1, send_2, send_3, pick_ref, pick_mask_ref, ends_ref,
    latent_ref, tops_ref, bottoms_ref, etop_ref, ebot_ref, live_ref, sems,
):
    moves = [
        pltpu.make_async_copy(src, dst, sems.at[i])
        for i, (src, dst) in enumerate((
            (tops_hbm, tops_ref), (bottoms_hbm, bottoms_ref), (latent_hbm, latent_ref),
            (etop_hbm, etop_ref), (ebot_hbm, ebot_ref), (live_hbm, live_ref),
            (pick_ref, out_pick), (pick_mask_ref, out_pick_mask),
            (send_0, out_0), (send_1, out_1), (send_2, out_2), (send_3, out_3),
            (ends_ref, out_ends),
        ))
    ]
    for move in moves[:6]:
        move.start()
    half = latent_ref.shape[0] // 2
    width = latent_ref.shape[1]
    sends = (send_0, send_1, send_2, send_3)
    moves[0].wait()
    moves[1].wait()
    for face in range(4):
        d, ref = face // 2, (tops_ref, bottoms_ref)[face % 2]
        bit, low = cut(ref[d : d + 1, :], half)
        pick_ref[face] = column_one_hot(low, half).T
        pick_mask_ref[face] = column_mask(bit, width)
    for move in moves[2:6]:
        move.wait()
    for move in moves[6:8]:
        move.start()
    pick_faces(latent_ref[...], pick_ref, pick_mask_ref, sends)
    faces = tops_ref.shape[1]
    slots = etop_ref.shape[1]
    lines = slots // width
    for d in range(2):
        live = lax.broadcasted_iota(I32, (1, slots), 1) < live_ref[0, d]
        etop = etop_ref[d : d + 1, :].astype(F32)
        ebot = jnp.where(live, ebot_ref[d : d + 1, :], -1).astype(F32)
        rows = [v[:, i * width : (i + 1) * width] for v in (etop, ebot) for i in range(lines)]
        ends = jnp.concatenate(rows, axis=0).astype(BF)
        ends_ref[d] = ends
        sends[PLACE[2 * d]][faces:, :] = ends
        sends[PLACE[2 * d + 1]][faces:, :] = ends
    for move in moves[8:]:
        move.start()
    for move in moves[6:]:
        move.wait()


def unpacked(ends):
    ends = ends.astype(F32)
    lines = ends.shape[0] // 2

    def row(start):
        parts = [ends[start + i : start + i + 1, :] for i in range(lines)]
        return jnp.concatenate(parts, axis=1).astype(I32)

    return row(0), row(lines)


def link_group(link, got_ref, ends_ref, tops_ref, bottoms_ref, half):
    d = link // 2
    owned = role_of(link) == 0
    faces = tops_ref.shape[1]
    width = got_ref.shape[1]
    etop, ebot = unpacked(jnp.where(owned, ends_ref[d], got_ref[faces:, :]))
    face = jnp.where(owned, tops_ref[d : d + 1, :], bottoms_ref[d : d + 1, :])
    here = column_one_hot(jnp.where(owned, etop, ebot), faces)
    there = column_one_hot(jnp.where(owned, ebot, etop), faces)
    bit, low = cut(face, half)
    lines = jnp.concatenate([low, bit, jnp.zeros((6, faces), I32)], axis=0)
    rows = dot(lines.astype(F32).astype(BF), here).astype(I32)
    low, bit = rows[0:1, :], rows[1:2, :]
    ones = column_one_hot(jnp.where(ebot >= 0, low, -1), half)
    gather = jnp.concatenate([here, there], axis=0).T
    return gather, jnp.where(owned, ones, -ones), column_mask(bit, width)


def link_first(step, link, got_ref, gather, ends_w_ref, biases_ref, table_ref, ahead_ref):
    role = role_of(link)
    faces = table_ref.shape[1]
    far = dot(got_ref[0:faces, :], ends_w_ref[step, 1 - role]).astype(BF)
    if step > 0:
        y = dot(gather[:, faces:], far) + ahead_ref[link]
    else:
        table = jnp.concatenate([table_ref[link], far], axis=0)
        y = dot(gather, table) + biases_ref[0, step : step + 1, :]
    return half_silu(y).astype(BF)


def second_layer(first, weight, bias):
    parts = [
        half_silu(dot(first[a : a + CUT], weight) + bias).astype(BF)
        for a in range(0, first.shape[0], CUT)
    ]
    return jnp.concatenate(parts, axis=0)


def placed(places, values):
    parts = []
    for a in range(0, places[0].shape[0], CUT):
        part = None
        for place, value in zip(places, values):
            product = dot(place[a : a + CUT], value)
            part = product if part is None else part + product
        parts.append(part)
    return jnp.concatenate(parts, axis=0)


def link_sums(step, links, gots, groups, ends_w_ref, hidden_ref, biases_ref, table_ref, ahead_ref):
    width = ends_w_ref.shape[2]
    wide = width * len(links)
    first = [
        link_first(step, link, got, group[0], ends_w_ref, biases_ref, table_ref, ahead_ref)
        for link, got, group in zip(links, gots, groups)
    ]
    bias = biases_ref[1, step : step + 1, :]
    second = second_layer(
        jnp.concatenate(first, axis=1),
        hidden_ref[step, 0:wide, 0:wide],
        jnp.concatenate([bias] * len(links), axis=1),
    )
    values = [
        by_half(second[:, i * width : (i + 1) * width], group[2]) for i, group in enumerate(groups)
    ]
    return placed([group[1] for group in groups], values)


def prepared(step, links, got_refs, refs, half):
    count = 3 * len(links)
    if step > 0:
        kept, rest = refs[:count], refs[count:]
    else:
        kept, rest = refs[-count:], refs[3:-count]
        for i, (link, got_ref) in enumerate(zip(links, got_refs)):
            for ref, value in zip(kept[3 * i :], link_group(link, got_ref, *refs[:3], half)):
                ref[...] = value
    return [tuple(ref[...] for ref in kept[i : i + 3]) for i in range(0, count, 3)], rest


def setup_kernel(
    nbr_ref, weights_ref, nodes_ref, raw_biases_ref,
    pick_ref, spread_ref, mask_ref, ends_w_ref, hidden_ref, join_ref, out_w_ref, biases_ref,
):
    half = spread_ref.shape[0]
    width = mask_ref.shape[1]
    rows = nbr_ref.shape[1]
    for k in range(nbr_ref.shape[0]):
        here = slice(k * rows, (k + 1) * rows)
        bit, low = cut(nbr_ref[k : k + 1, :], half)
        ones = column_one_hot(low, half)
        pick_ref[here, :] = ones.T
        spread_ref[:, here] = -ones
        mask_ref[here, :] = column_mask(bit, width)
    biases_ref[...] = raw_biases_ref[...] * 0.5
    zero = jnp.zeros((width, width), BF)
    for step in range(weights_ref.shape[0]):
        ends_w_ref[step, 0] = weights_ref[step, 0] * BF(0.5)
        ends_w_ref[step, 1] = weights_ref[step, 1] * BF(0.5)
        hidden = weights_ref[step, 2] * BF(0.5)
        hidden_ref[step] = jnp.concatenate(
            [jnp.concatenate([hidden, zero], axis=1), jnp.concatenate([zero, hidden], axis=1)],
            axis=0,
        )
        fold = dot(weights_ref[step, 3], nodes_ref[step, 1]).astype(BF)
        join_ref[step] = jnp.concatenate([nodes_ref[step, 0], fold], axis=0) * BF(0.5)
        out_w_ref[step] = nodes_ref[step, 2]


def inner_kernel(
    step, latent_ref, send_0, send_1, send_2, send_3, ends_w_ref, hidden_ref, biases_ref,
    pick_ref, spread_ref, mask_ref, *refs,
):
    rows, width = latent_ref.shape
    half = rows // 2
    sends = (send_0, send_1, send_2, send_3)
    if step > 0:
        gather_refs, (total_ref, table_ref, ahead_ref) = refs[:4], refs[4:]
    else:
        total_ref, table_ref = refs
    faces = table_ref.shape[1]
    for link in range(4):
        face = sends[PLACE[link]][0:faces, :]
        table_ref[link] = dot(face, ends_w_ref[step, role_of(link)]).astype(BF)
    latent = latent_ref[...]
    source = dot(latent, ends_w_ref[step, 0]) + biases_ref[0, step : step + 1, :]
    table = halves(dot(latent, ends_w_ref[step, 1]).astype(BF))
    c1 = biases_ref[1, step : step + 1, :]
    c1 = jnp.concatenate([c1, c1], axis=1)
    fanout = pick_ref.shape[0] // rows
    total = None
    ended = None
    for pair in range(0, fanout, 2):
        here = [slice(k * rows, (k + 1) * rows) for k in (pair, pair + 1)]
        first = [
            half_silu(choose(dot(pick_ref[k, :], table), mask_ref[k, :]) + source).astype(BF)
            for k in here
        ]
        first = jnp.concatenate(first, axis=1)
        second = [
            half_silu(dot(first[a : a + CUT], hidden_ref[step]) + c1) for a in range(0, rows, CUT)
        ]
        started = jnp.concatenate([q[:, :width] + q[:, width:] for q in second], axis=0)
        total = started if total is None else total + started
        second = jnp.concatenate([q.astype(BF) for q in second], axis=0)
        values = [
            by_half(second[:, i * width : (i + 1) * width], mask_ref[k, :])
            for i, k in enumerate(here)
        ]
        part = jnp.concatenate(
            [dot(spread_ref[a : a + CUT, here[0]], values[0])
             + dot(spread_ref[a : a + CUT, here[1]], values[1]) for a in range(0, half, CUT)],
            axis=0,
        )
        ended = part if ended is None else ended + part
    total_ref[0:half, :] = total[0:half] + ended[:, :width]
    total_ref[half:, :] = total[half:] + ended[:, width:]
    if step > 0:
        c0 = biases_ref[0, step : step + 1, :]
        for link, ref in enumerate(gather_refs):
            ahead_ref[link] = dot(ref[:, 0:faces], table_ref[link]) + c0


def cross_kernel(step, links, total_ref, *refs):
    rows, width = total_ref.shape
    half = rows // 2
    gots, refs = refs[: len(links)], refs[len(links) :]
    nets, refs = refs[: 4 + (step > 0)], refs[4 + (step > 0) :]
    groups, (out_ref,) = prepared(step, links, gots, refs, half)
    ahead_ref = nets[4] if step > 0 else None
    both = link_sums(step, links, gots, groups, *nets[:4], ahead_ref)
    out_ref[0:half, :] = total_ref[0:half, :] + both[:, :width]
    out_ref[half:, :] = total_ref[half:, :] + both[:, width:]


def last_kernel(step, links, last, total_ref, *refs):
    rows, width = total_ref.shape
    half = rows // 2
    gots, refs = refs[: len(links)], refs[len(links) :]
    nets, refs = refs[: 4 + (step > 0)], refs[4 + (step > 0) :]
    (latent_ref, join_ref, out_w_ref), refs = refs[:3], refs[3:]
    groups, rest = prepared(step, links, gots, refs, half)
    ahead_ref = nets[4] if step > 0 else None
    biases_ref = nets[2]
    both = link_sums(step, links, gots, groups, *nets[:4], ahead_ref)
    arrived = total_ref[...] + jnp.concatenate([both[:, :width], both[:, width:]], axis=0)
    if last:
        out_hbm, held_ref, sems = rest
        moves = []
        for i, a in enumerate((0, half)):
            here = pl.ds(a, half)
            old = latent_ref[a : a + half, :]
            joined = jnp.concatenate([old, arrived[a : a + half].astype(BF)], axis=1)
            update = half_silu(dot(joined, join_ref[step]) + biases_ref[2, step : step + 1, :])
            held_ref[a : a + half, :] = (
                old.astype(F32) + dot(update.astype(BF), out_w_ref[step])
            ).astype(BF)
            moves.append(pltpu.make_async_copy(held_ref.at[here], out_hbm.at[here], sems.at[i]))
            moves[i].start()
        for move in moves:
            move.wait()
    else:
        latent = latent_ref[...]
        joined = jnp.concatenate([latent, arrived.astype(BF)], axis=1)
        update = half_silu(dot(joined, join_ref[step]) + biases_ref[2, step : step + 1, :]).astype(BF)
        latent = (latent.astype(F32) + dot(update, out_w_ref[step])).astype(BF)
        pick_ref, pick_mask_ref, out_ref = rest[:3]
        out_ref[...] = latent
        pick_faces(latent, pick_ref, pick_mask_ref, rest[3:7])


def local(
    latent,
    neighbours,
    top_rows,
    bottom_rows,
    edge_top,
    edge_bottom,
    live_count,
    edge_weights,
    node_weights,
    biases,
):
    latent_now = latent[0, 0]
    rows, width = latent_now.shape
    half = rows // 2
    nbr = neighbours[0, 0]
    tops = top_rows[0, 0]
    bottoms = bottom_rows[0, 0]
    etop = edge_top[0, 0]
    ebot = edge_bottom[0, 0]
    live = live_count.T
    bias_rows = jnp.swapaxes(biases, 0, 1)
    fanout = nbr.shape[0]
    faces = tops.shape[1]
    slots = etop.shape[1]
    steps = edge_weights.shape[0]
    like = jax.ShapeDtypeStruct
    face = like((faces, width), BF)
    lines = 2 * (slots // width)
    packed = like((faces + lines, width), BF)
    *sends, pick, pick_mask, ends = call(
        first_kernel,
        [packed] * 4
        + [like((4, faces, half), BF), like((4, faces, width), BF), like((2, lines, width), BF)],
        (latent_now, tops, bottoms, etop, ebot, live),
        in_specs=[HBM] * 6,
        out_specs=[HBM] * 7,
        scratch=[pltpu.VMEM(packed.shape, BF)] * 4 + [
            pltpu.VMEM((4, faces, half), BF), pltpu.VMEM((4, faces, width), BF),
            pltpu.VMEM((2, lines, width), BF),
            pltpu.VMEM((rows, width), BF), pltpu.VMEM(tops.shape, I32),
            pltpu.VMEM(tops.shape, I32), pltpu.VMEM(etop.shape, I32), pltpu.VMEM(etop.shape, I32),
            pltpu.SMEM(live.shape, I32), pltpu.SemaphoreType.DMA((13,)),
        ],
        name="first",
        grant=54 << 20,
    )
    group_like = [
        like((slots, 2 * faces), BF), like((half, slots), BF), like((slots, width), BF)
    ]
    groups = {}
    for step in range(steps):
        starting, last = step == 0, step == steps - 1
        near_x, far_x, near_y, far_y = (sends[place] for place in PLACE)
        got = {
            FAR_Y: swapped(far_y, "gy", 1),
            FAR_X: swapped(far_x, "gx", 1),
            NEAR_Y: swapped(near_y, "gy", 0),
            NEAR_X: swapped(near_x, "gx", 0),
        }
        if starting:
            made = call(
                setup_kernel,
                [like((fanout * rows, half), BF), like((half, fanout * rows), BF),
                 like((fanout * rows, width), BF),
                 like((steps, 2, width, width), BF), like((steps, 2 * width, 2 * width), BF),
                 like((steps, 2 * width, width), BF), like((steps, width, width), BF),
                 like(bias_rows.shape, F32)],
                (nbr, edge_weights, node_weights, bias_rows),
                name="setup",
            )
            inner, (ends_w, hidden, join, out_w, half_biases) = made[:3], made[3:]
            edge_net = (ends_w, hidden, half_biases)
        gathers = () if starting else tuple(groups[link][0] for link in range(4))
        total, *tables = call(
            functools.partial(inner_kernel, step),
            [like((rows, width), F32), like((4, faces, width), BF)]
            + ([] if starting else [like((4, slots, width), F32)]),
            (latent_now, *sends, *edge_net, *inner, *gathers),
            name="inner",
        )
        for links in VISITS:
            final = links == VISITS[-1]
            kernel = functools.partial(cross_kernel, step, links)
            outs = [like((rows, width), F32)]
            operands = [total, *(got[link] for link in links), *edge_net, *tables]
            if final:
                kernel = functools.partial(last_kernel, step, links, last)
                outs = [like((rows, width), BF)] + ([] if last else [face] * 4)
                operands += [latent_now, join, out_w]
            plain = len(outs)
            if starting:
                outs += group_like * len(links)
                operands += [ends, tops, bottoms]
            else:
                operands += [part for link in links for part in groups[link]]
            if final and not last:
                operands += [pick, pick_mask]
            total, *made = call(
                kernel, outs, operands,
                out_specs=[HBM] if final and last else None,
                scratch=[pltpu.VMEM((rows, width), BF), pltpu.SemaphoreType.DMA((2,))]
                if final and last else (),
                name="update" if final else "cross",
            )
            if starting:
                for k, link in enumerate(links):
                    groups[link] = made[plain - 1 + 3 * k :][:3]
            if final:
                latent_now, sends = total, made[: plain - 1]
    return latent_now[None, None]


def solution(mesh):
    return jax.shard_map(
        local,
        mesh=mesh,
        in_specs=(
            P("gx", "gy", None, None),
            P("gx", "gy", None, None),
            P("gx", "gy", None, None),
            P("gx", "gy", None, None),
            P("gx", "gy", None, None),
            P("gx", "gy", None, None),
            P(None, ("gx", "gy")),
            P(),
            P(),
            P(),
        ),
        out_specs=P("gx", "gy", None, None),
        check_vma=False,
    )
```
